32 devices in a mesh: segment: 2 (over core), expert: 16 (over z, y, x).
Axes of the slice: x: 2, y: 2, z: 4, core: 2. Of those that a mesh axis runs over, the one named last changes fastest.
Arguments:
- tokens: bfloat16 [2, 256, 4096], P(None, 'expert'), may hold values from -6 to 6
- expert_ids: int32 [2, 2, 256, 8], P('segment', None, 'expert'), may hold values from 0 to 15, all different within a row; in each aligned block of 16 rows (0 to 15, 16 to 31, ..., all dimensions but the last counted through in order) at most 16 rows name the same one
- gate_weights: float32 [2, 2, 256, 8], P('segment', None, 'expert'), may hold values from 0.05 to 0.5
- norm_gain: float32 [2, 4096], P('segment'), may hold values from 0.25 to 1.75
- w_gate: bfloat16 [2, 16, 4096, 768], P('segment', 'expert'), may hold values from -0.09375 to 0.09375
- w_up: bfloat16 [2, 16, 4096, 768], P('segment', 'expert'), may hold values from -0.09375 to 0.09375
- w_down: bfloat16 [2, 16, 768, 4096], P('segment', 'expert'), may hold values from -0.21875 to 0.21875
Outputs:
- section_out: bfloat16 [2, 2, 256, 4096], P('segment', None, 'expert')
The draws below stay inside these ranges and needn't reach their ends.
Inputs may be any that keep to these rules, and one draw needn't show every extreme that they name: `expert_ids`: each row names 8 different experts. In each aligned block of 16 rows (the rows of one device for one section and micro-batch) no expert is named more than 16 times, a bound that some block reaches.
All inputs are finite; a program needn't handle non-finite values.
Results may differ from the reference program's by a relative error of at most 0.0059.
Values may be sent and summed in bfloat16 or wider, within the bound.
A program may use at most 128 MiB of HBM per device.

```python
import math
import jax
import jax.numpy as jnp
import numpy as np
from jax import lax

D = 4096
FF = 768
TOP = 8
MICRO = 2
TOK_DEV = 16
SEGMENTS = 2
EXPERTS = 16
TOKENS = 256
CAP = 16
N_SEGMENT = 2
N_EXPERT = 16


def block_scale(key, shape, split, least, high):
    def one(dim, blocks):
        steps = jax.random.uniform(jax.random.fold_in(jax.random.fold_in(key, 6), dim), (blocks,), jnp.float32, least / len(split), high / len(split))
        return jnp.repeat(jnp.exp(steps), shape[dim] // blocks).reshape((-1,) + (1,) * (len(shape) - dim - 1))

    factor_of = one(*split[0])
    for cut in split[1:]:
        factor_of = factor_of * one(*cut)
    return factor_of


def shared_out(own_key, own, number, rows, count, top, limit, skew):
    ranking = jax.random.permutation(own_key, count)
    crowded, usual = load_shares(count, rows * top, limit, skew, True), load_shares(count, rows * top, limit, skew, False)
    places = jnp.arange(count)

    def named(sizes, offset_by):
        used = int((sizes > 0).sum())
        fixed = max(1, used // 4)
        moved = fixed + (places - fixed + offset_by * (used - fixed)) % max(1, count - fixed)
        return jnp.zeros((count,), jnp.int32).at[ranking[jnp.where(places < fixed, places, moved)]].set(jnp.asarray(sizes, jnp.int32))

    sizes = jnp.where(number % 4 == 0, named(crowded, number // 4), named(usual, number - number // 4 - 1))
    mixed = jax.random.permutation(jax.random.fold_in(own, 3), count)
    source_of, receiver = mixed[0:count // 2 * 2:2], mixed[1:count // 2 * 2:2]
    margin = jnp.minimum(sizes[source_of] - 1, limit - sizes[receiver]) // 2
    margin = jnp.where((source_of == ranking[0]) | (receiver == ranking[0]) | (sizes[receiver] == 0), 0, jnp.maximum(margin, 0))
    moved = jax.random.randint(jax.random.fold_in(own, 4), (count // 2,), 0, 1 << 20) % (margin + 1)
    sizes = sizes.at[source_of].add(-moved).at[receiver].add(moved)
    members = jnp.searchsorted(jnp.cumsum(sizes), jnp.arange(rows * top), side="right").astype(jnp.int32)
    listing = members.reshape(top, rows).T
    listing = listing[jax.random.permutation(jax.random.fold_in(own, 1), rows)]
    offset_by = jax.random.randint(jax.random.fold_in(own, 2), (rows, 1), 0, top)
    return jnp.take_along_axis(listing, (jnp.arange(top)[None, :] + offset_by) % top, axis=1)


def load_shares(count, total, reach, skew, full):
    loads = [(1 << 20) // math.isqrt(grade ** skew) + 1 for grade in range(1, count + 1)]
    largest = reach if full else min(reach, max(-(-total // count), total * loads[0] // sum(loads)))
    least = 1 if total - largest >= count - 1 else 0
    counts, surplus = [largest] + [least] * (count - 1), total - largest - least * (count - 1)
    while surplus > 0:
        movable = [i for i in range(1, count) if counts[i] < largest] or [i for i in range(1, count) if counts[i] < reach]
        mass, left = sum([loads[i] for i in movable]), surplus
        for i in movable:
            addition = min(reach - counts[i], max(1, left * loads[i] // mass), surplus)
            counts[i] = counts[i] + addition
            surplus = surplus - addition
    return np.array(counts)


def normal_values(own_key, extent, scale, bound, pieces=(), kind=jnp.bfloat16):
    level = block_scale(own_key, extent, pieces, -0.22, 0.18) if pieces else 1.0
    values = jax.random.normal(own_key, extent, jnp.float32) * scale * level
    return jnp.minimum(jnp.maximum(values, -bound), bound).astype(kind)


def setup_inputs(seed: int = 0) -> dict:
    streams_of = jax.random.split(jax.random.key(seed), 8)
    tokens = normal_values(streams_of[0], (MICRO, TOKENS, D), 1.0, 6.0, ((1, 16),))
    expert_ids_keys = jax.random.split(jax.random.fold_in(streams_of[1], 1), SEGMENTS * MICRO * TOKENS // TOK_DEV)
    expert_ids_turns = jax.random.permutation(jax.random.fold_in(streams_of[1], 3), SEGMENTS * MICRO * TOKENS // TOK_DEV)
    expert_ids = jax.vmap(lambda own, number: shared_out(jax.random.fold_in(streams_of[1], 2), own, number, TOK_DEV, EXPERTS, TOP, CAP, 2))(expert_ids_keys, expert_ids_turns).reshape((SEGMENTS, MICRO, TOKENS, TOP))
    gate_weights = jnp.clip(jnp.exp(math.log(0.5) - 2.3025851 * jax.random.uniform(streams_of[2], (SEGMENTS, MICRO, TOKENS, TOP), jnp.float32) ** block_scale(streams_of[2], (SEGMENTS, MICRO, TOKENS, TOP), ((0, 2), (2, 16)), -0.2, 0.2)), 0.05, 0.5)
    norm_gain = jnp.clip(1.0 + 0.15 * jax.random.normal(streams_of[3], (SEGMENTS, D), jnp.float32), 0.25, 1.75)
    w_gate = normal_values(streams_of[4], (SEGMENTS, EXPERTS, D, FF), D ** -0.5, 0.09375, ((0, 2), (1, 16)))
    w_up = normal_values(streams_of[5], (SEGMENTS, EXPERTS, D, FF), D ** -0.5, 0.09375, ((0, 2), (1, 16)))
    w_down = normal_values(streams_of[6], (SEGMENTS, EXPERTS, FF, D), FF ** -0.5, 0.21875, ((0, 2), (1, 16)))
    return {"tokens": tokens, "expert_ids": expert_ids, "gate_weights": gate_weights, "norm_gain": norm_gain, "w_gate": w_gate, "w_up": w_up, "w_down": w_down}


def norm_rows(current, gain):
    values = current.astype(jnp.float32)
    scaled = values * lax.rsqrt(lax.optimization_barrier(jnp.mean(values * values, axis=-1, keepdims=True)) + 1e-06)
    return (scaled * gain.astype(jnp.float32)).astype(jnp.bfloat16)

def expert_apply(operands):
    row_block, gate_mat, up_mat, down_mat = operands
    gate_part = jnp.dot(row_block, gate_mat, preferred_element_type=jnp.float32)
    up_part = jnp.dot(row_block, up_mat, preferred_element_type=jnp.float32)
    hidden = (jax.nn.silu(gate_part) * up_part).astype(jnp.bfloat16)
    return jnp.dot(hidden, down_mat, preferred_element_type=jnp.float32).astype(jnp.bfloat16)

def one_layer(current, routes, weighting, gain, gate_all, up_all, down_all):
    normed = norm_rows(current, gain)
    blocks = routes.reshape(N_EXPERT, TOK_DEV * TOP).astype(jnp.int32)
    onehot = (blocks[:, :, None] == jnp.arange(EXPERTS, dtype=jnp.int32)[None, None, :]).astype(jnp.int32)
    ranks = lax.optimization_barrier(jnp.sum(jnp.cumsum(onehot, axis=1) * onehot, axis=2)) - 1
    source = jnp.arange(N_EXPERT, dtype=jnp.int32)[:, None]
    index = ((blocks * N_EXPERT + source) * CAP + ranks).reshape(-1).astype(jnp.int32)
    spread = jnp.repeat(normed, TOP, axis=0)
    dispatch_rows = jnp.zeros((EXPERTS * N_EXPERT * CAP, D), jnp.bfloat16).at[index].set(spread)
    served = lax.map(expert_apply, (dispatch_rows.reshape(EXPERTS, N_EXPERT * CAP, D), gate_all, up_all, down_all))
    picked = served.reshape(-1, D)[index].reshape(TOKENS, TOP, D)
    mixed = current.astype(jnp.float32) + lax.optimization_barrier(jnp.sum(weighting[:, :, None].astype(jnp.float32) * picked.astype(jnp.float32), axis=1))
    return mixed.astype(jnp.bfloat16)

def reference(tokens, expert_ids, gate_weights, norm_gain, w_gate, w_up, w_down):
    inputs = [tokens[micro_no] for micro_no in range(MICRO)]
    segment_outs = []
    for segment_no in range(N_SEGMENT):
        layer_outs = []
        for micro_no in range(MICRO):
            layer_outs.append(one_layer(inputs[micro_no], expert_ids[segment_no, micro_no], gate_weights[segment_no, micro_no], norm_gain[segment_no], w_gate[segment_no], w_up[segment_no], w_down[segment_no]))
        segment_outs.append(jnp.stack(layer_outs))
        inputs = layer_outs
    return jnp.stack(segment_outs)
```

```python
import functools

import jax
import jax.numpy as jnp
from jax import lax
from jax.experimental import pallas as pl
from jax.experimental.pallas import tpu as pltpu
from jax.sharding import PartitionSpec as P

PLANE = 4
CHUNKS = 4
LANES = 128
VMEM_BYTES = 60 * 1024 * 1024
MESH = pl.DeviceIdType.MESH


def vmem_need(micro, tok_dev, width, ff, groups):
    rows = tok_dev * groups
    weights = 3 * width * ff * 2
    features = 2 * micro * rows * width * 2
    landing = micro * (rows // PLANE) * width * 2 * 4 + micro * tok_dev * width * 2 * 6
    hidden = rows * ff * (8 + 2) + rows * LANES * 4
    return weights + features + landing + hidden


def relay_kernel(
    micro, segments, groups, tok_dev, width, ff, chunks,
    tok, ids, gw, gain, wg, wu, wd, out,
    xg, cur, outb, part, r1, r2, r3, zb, gb, wgv, wuv, wdv, acc, hid,
    wsem, zs, zr, xs, xr, fs, fr, r1s, r1r, r2s, r2r, r3s, r3r, cs, cr,
):
    depth = groups // PLANE
    wide = width // chunks
    bundle = depth * tok_dev
    half = bundle // 2
    seg = lax.axis_index("segment")
    me = lax.axis_index("expert")
    yx = me % PLANE
    z = me // PLANE
    xn = yx + 1 - 2 * (yx % 2)
    yn = yx + 2 - 4 * (yx // 2)
    across = PLANE - 1 - yx
    x_dev = z * PLANE + xn
    y_dev = z * PLANE + yn

    def rows(start, size):
        return pl.ds(pl.multiple_of(start, 16), size)

    def peer(d):
        return (z + d) % depth

    own_rows = rows((yx * depth + z) * tok_dev, tok_dev)

    def bundle_rows(which):
        return rows(which * bundle, bundle)

    def first_rows(which):
        return rows(which * bundle, half)

    def last_rows(which):
        return rows(which * bundle + half, half)

    def send(src, dst, s, r, dev):
        return pltpu.make_async_remote_copy(
            src_ref=src, dst_ref=dst, send_sem=s, recv_sem=r, device_id=(seg, dev), device_id_type=MESH
        )

    def feature(m, c):
        return gb if c is None else xg.at[m, c]

    def slot(c):
        return chunks if c is None else c

    def z_copy(m, c, d):
        ref = feature(m, c).at[own_rows]
        return send(ref, ref, zs.at[m, slot(c), d - 1], zr.at[m, slot(c), d - 1], peer(d) * PLANE + yx)

    def xy_copy(m, c, a):
        ref = feature(m, c).at[bundle_rows(yx)]
        return send(ref, ref, xs.at[m, slot(c), a], xr.at[m, slot(c), a], (x_dev, y_dev)[a])

    def f_copy(m, c, a):
        ref = feature(m, c).at[(first_rows(xn), last_rows(yn))[a]]
        return send(ref, ref, fs.at[m, slot(c), a], fr.at[m, slot(c), a], (y_dev, x_dev)[a])

    def z_send(m, c):
        for d in range(1, depth):
            z_copy(m, c, d).start()

    def xy_send(m, c):
        for d in range(1, depth):
            z_copy(m, c, d).wait_recv()
        for a in range(2):
            xy_copy(m, c, a).start()

    def f_send(m, c):
        for a in range(2):
            xy_copy(m, c, a).wait_recv()
            f_copy(m, c, a).start()

    def f_wait(m, c):
        for a in range(2):
            f_copy(m, c, a).wait_recv()

    def r1_copy(m, c, a):
        ref = part.at[m, c, (first_rows(across), last_rows(across))[a]]
        return send(ref, r1.at[m, c, a], r1s.at[m, c, a], r1r.at[m, c, a], (y_dev, x_dev)[a])

    def r2_copy(m, c, a):
        ref = part.at[m, c, bundle_rows((xn, yn)[a])]
        return send(ref, r2.at[m, c, a], r2s.at[m, c, a], r2r.at[m, c, a], (x_dev, y_dev)[a])

    def r3_copy(m, c, d):
        ref = zb.at[m, c, rows(peer(d) * tok_dev, tok_dev)]
        return send(ref, r3.at[m, c, d - 1], r3s.at[m, c, d - 1], r3r.at[m, c, d - 1], peer(d) * PLANE + yx)

    def relay_copy(m, c):
        return pltpu.make_async_remote_copy(
            src_ref=outb.at[m, c], dst_ref=cur.at[m, c], send_sem=cs.at[m, c], recv_sem=cr.at[m, c],
            device_id=(1 - seg, me), device_id_type=MESH,
        )

    f32 = jnp.float32

    def r2_send(m, c):
        for a in range(2):
            r1_copy(m, c, a).wait_recv()
            into = (first_rows(xn), last_rows(yn))[a]
            part[m, c, into] = (part[m, c, into].astype(f32) + r1[m, c, a].astype(f32)).astype(jnp.bfloat16)
            r2_copy(m, c, a).start()

    def r3_send(m, c):
        for a in range(2):
            r2_copy(m, c, a).wait_recv()
        total = part[m, c, bundle_rows(yx)].astype(f32) + r2[m, c, 0].astype(f32) + r2[m, c, 1].astype(f32)
        zb[m, c] = total.astype(jnp.bfloat16)
        for d in range(1, depth):
            r3_copy(m, c, d).start()

    def finish(m, c):
        for d in range(1, depth):
            r3_copy(m, c, d).wait_recv()
        inside = rows(z * tok_dev, tok_dev)
        total = part[m, c, own_rows].astype(f32) + r2[m, c, 0, inside].astype(f32) + r2[m, c, 1, inside].astype(f32)
        for d in range(1, depth):
            total = total + r3[m, c, d - 1].astype(f32)
        value = (cur[m, c].astype(f32) + total).astype(jnp.bfloat16)
        outb[m, c] = value
        out[m, :, pl.ds(pl.multiple_of(c * wide, LANES), wide)] = value

        @pl.when(seg == 0)
        def _():
            relay_copy(m, c).start()

    def weight_copy(which, c):
        src = (
            wg.at[rows(c * wide, wide)], wu.at[rows(c * wide, wide)],
            wd.at[:, pl.ds(pl.multiple_of(c * wide, LANES), wide)],
        )[which]
        return pltpu.make_async_copy(src, (wgv, wuv, wdv)[which].at[c], wsem.at[which, c])

    def up_chunk(m, c):
        f_wait(m, c)

        @pl.when(m == 0)
        def _():
            weight_copy(0, c).wait()
            weight_copy(1, c).wait()

        x = xg[m, c]
        gate = jnp.dot(x, wgv[c], preferred_element_type=f32)
        up = jnp.dot(x, wuv[c], preferred_element_type=f32)

        @pl.when(c == 0)
        def _():
            acc[0] = gate
            acc[1] = up

        @pl.when(c > 0)
        def _():
            acc[0] += gate
            acc[1] += up

    experts = groups

    def down_chunk(m, c):
        @pl.when(m == 0)
        def _():
            weight_copy(2, c).wait()

        lane = lax.broadcasted_iota(jnp.int32, (groups * tok_dev, LANES), 1)
        gate = jnp.sum(jnp.where(lane == m * experts + me, gb[...], 0.0), axis=1, keepdims=True)
        value = jnp.dot(hid[...], wdv[c], preferred_element_type=f32)
        part[m, c] = (value * gate).astype(jnp.bfloat16)
        for a in range(2):
            r1_copy(m, c, a).start()

    def take_in(m):
        @pl.when(seg == 0)
        def _():
            for c in range(chunks):
                cur[m, c] = tok[m, :, c * wide:(c + 1) * wide]

        @pl.when(seg > 0)
        def _():
            for c in range(chunks):
                relay_copy(m, c).wait_recv()

        square = jnp.zeros((tok_dev, 1), f32)
        for c in range(chunks):
            value = cur[m, c].astype(f32)
            square = square + jnp.sum(value * value, axis=1, keepdims=True)
        scale = lax.rsqrt(square / width + 1e-6)
        for c in range(chunks):
            value = cur[m, c].astype(f32) * scale * gain[:, c * wide:(c + 1) * wide]
            xg[m, c, own_rows] = value.astype(jnp.bfloat16)
            z_send(m, c)

    barrier = pltpu.get_barrier_semaphore()
    partners = [(seg, peer(d) * PLANE + yx) for d in range(1, depth)]
    partners += [(seg, x_dev), (seg, y_dev), (1 - seg, me)]
    for partner in partners:
        pl.semaphore_signal(barrier, inc=1, device_id=partner, device_id_type=MESH)
    for c in range(chunks):
        weight_copy(0, c).start()
        weight_copy(1, c).start()
    for c in range(chunks):
        weight_copy(2, c).start()

    lane = lax.broadcasted_iota(jnp.int32, (tok_dev, LANES), 1)
    gates = jnp.zeros((tok_dev, LANES), f32)
    for m in range(micro):
        for k in range(ids.shape[-1]):
            hit = lane == ids[m, :, k:k + 1] + m * experts
            gates = gates + jnp.where(hit, gw[m, :, k:k + 1], 0.0)
    gb[own_rows] = gates
    pl.semaphore_wait(barrier, len(partners))

    def stage(m, carry):
        @pl.when(m < micro)
        def _():
            take_in(m)

        @pl.when(m == 0)
        def _():
            z_send(0, None)

        def step(t, carry):
            new = m < micro
            old = m > 0

            @pl.when(new & (t < chunks))
            def _():
                xy_send(m, t)

            @pl.when((m == 0) & (t == 0))
            def _():
                xy_send(0, None)

            @pl.when(old & (t < chunks))
            def _():
                down_chunk(m - 1, t)

            @pl.when(new & (t >= 1) & (t < chunks + 1))
            def _():
                f_send(m, t - 1)

            @pl.when((m == 0) & (t == 1))
            def _():
                f_send(0, None)

            @pl.when(old & (t >= 1) & (t < chunks + 1))
            def _():
                r2_send(m - 1, t - 1)

            @pl.when(old & (t >= 2) & (t < chunks + 2))
            def _():
                r3_send(m - 1, t - 2)

            @pl.when(new & (t >= 2) & (t < chunks + 2))
            def _():
                up_chunk(m, t - 2)

            @pl.when((m == 0) & (t == 2))
            def _():
                f_wait(0, None)

            @pl.when(old & (t >= 3))
            def _():
                finish(m - 1, t - 3)

            return carry

        lax.fori_loop(0, chunks + 3, step, 0)

        @pl.when(m < micro)
        def _():
            gate = acc[0]
            hid[...] = (gate * jax.nn.sigmoid(gate) * acc[1]).astype(jnp.bfloat16)

        return carry

    lax.fori_loop(0, micro + 1, stage, 0)

    def sent(m, c, with_return):
        for d in range(1, depth):
            z_copy(m, c, d).wait_send()
        for a in range(2):
            xy_copy(m, c, a).wait_send()
            f_copy(m, c, a).wait_send()
        if with_return:
            for a in range(2):
                r1_copy(m, c, a).wait_send()
                r2_copy(m, c, a).wait_send()
            for d in range(1, depth):
                r3_copy(m, c, d).wait_send()

            @pl.when(seg == 0)
            def _():
                relay_copy(m, c).wait_send()

    def drain(i, carry):
        sent(i // chunks, i % chunks, True)
        return carry

    lax.fori_loop(0, micro * chunks, drain, 0)
    sent(0, None, False)


def fused(tokens, expert_ids, gate_weights, norm_gain, w_gate, w_up, w_down):
    micro, tok_dev, width = tokens.shape
    ff = w_gate.shape[-1]
    groups = lax.axis_size("expert")
    segments = lax.axis_size("segment")
    depth = groups // PLANE
    rows = groups * tok_dev
    bundle = depth * tok_dev
    chunks = CHUNKS
    wide = width // chunks
    bf16 = jnp.bfloat16
    dma = pltpu.SemaphoreType.DMA
    vmem = pl.BlockSpec(memory_space=pltpu.VMEM)
    hbm = pl.BlockSpec(memory_space=pl.ANY)
    scratch = [
        pltpu.VMEM((micro, chunks, rows, wide), bf16),
        pltpu.VMEM((micro, chunks, tok_dev, wide), bf16),
        pltpu.VMEM((micro, chunks, tok_dev, wide), bf16),
        pltpu.VMEM((micro, chunks, rows, wide), bf16),
        pltpu.VMEM((micro, chunks, 2, bundle // 2, wide), bf16),
        pltpu.VMEM((micro, chunks, 2, bundle, wide), bf16),
        pltpu.VMEM((micro, chunks, depth - 1, tok_dev, wide), bf16),
        pltpu.VMEM((micro, chunks, bundle, wide), bf16),
        pltpu.VMEM((rows, LANES), jnp.float32),
        pltpu.VMEM((chunks, wide, ff), bf16),
        pltpu.VMEM((chunks, wide, ff), bf16),
        pltpu.VMEM((chunks, ff, wide), bf16),
        pltpu.VMEM((2, rows, ff), jnp.float32),
        pltpu.VMEM((rows, ff), bf16),
        dma((3, chunks)),
    ]
    for count, kinds in ((chunks + 1, (depth - 1, 2, 2)), (chunks, (2, 2, depth - 1))):
        for kind in kinds:
            scratch += [dma((micro, count, kind))] * 2
    scratch += [dma((micro, chunks))] * 2
    result = pl.pallas_call(
        functools.partial(relay_kernel, micro, segments, groups, tok_dev, width, ff, chunks),
        out_shape=jax.ShapeDtypeStruct((micro, tok_dev, width), bf16),
        in_specs=[vmem, vmem, vmem, vmem, hbm, hbm, hbm],
        out_specs=vmem,
        scratch_shapes=scratch,
        compiler_params=pltpu.CompilerParams(
            collective_id=0, has_side_effects=True, vmem_limit_bytes=VMEM_BYTES
        ),
        cost_estimate=pl.CostEstimate(
            flops=micro * 6 * rows * width * ff, bytes_accessed=3 * width * ff * 2, transcendentals=micro * rows * ff
        ),
    )(tokens, expert_ids[0], gate_weights[0], norm_gain, w_gate[0, 0], w_up[0, 0], w_down[0, 0])
    return result[None]


def fits(tokens, expert_ids, w_gate):
    micro, tok_dev, width = tokens.shape
    groups = lax.axis_size("expert")
    return (
        lax.axis_size("segment") == 2
        and w_gate.shape[1] == 1
        and groups % PLANE == 0
        and groups > PLANE
        and (groups // PLANE) % 2 == 0
        and tok_dev % 16 == 0
        and width % (CHUNKS * LANES) == 0
        and micro * groups <= LANES
        and vmem_need(micro, tok_dev, width, w_gate.shape[3], groups) < VMEM_BYTES * 4 // 5
    )


def from_behind(value, axis, steps):
    count = lax.axis_size(axis)
    initial, last = (max(0, -steps), min(count, count - steps))
    return lax.ppermute(value, axis, [(source, source + steps) for source in range(initial, last)])


def norm_rows(current, gain):
    values = current.astype(jnp.float32)
    scaled = values * lax.rsqrt(jnp.mean(values * values, axis=-1, keepdims=True) + 1e-06)
    return (scaled * gain).astype(jnp.bfloat16)


def slot_index(routes, capacity, experts):
    flat = routes.reshape(-1)
    onehot = (flat[:, None] == jnp.arange(experts, dtype=jnp.int32)[None, :]).astype(jnp.int32)
    ranks = jnp.sum(jnp.cumsum(onehot, axis=0) * onehot, axis=1) - 1
    return (flat * capacity + ranks).reshape(routes.shape)


def expert_rows(received, weights):
    gate_all, up_all, down_all = weights
    row_block = received[:, 0].reshape(-1, received.shape[-1])
    gate_part = jnp.dot(row_block, gate_all[0], preferred_element_type=jnp.float32)
    up_part = jnp.dot(row_block, up_all[0], preferred_element_type=jnp.float32)
    hidden = (jax.nn.silu(gate_part) * up_part).astype(jnp.bfloat16)
    result = jnp.dot(hidden, down_all[0], preferred_element_type=jnp.float32).astype(jnp.bfloat16)
    outputs = [result.reshape(received.shape[0], received.shape[2], received.shape[3])]
    return jnp.stack(outputs, axis=1)


def serve_rows(received, weights):
    return lax.all_to_all(
        expert_rows(received, weights), "expert", split_axis=0, concat_axis=0, tiled=True
    )


def pick_rows(gathered, all_routes, member, local, capacity, groups):
    tok_dev = all_routes.shape[0] // groups
    top = all_routes.shape[1]
    blocks = all_routes.reshape(groups, tok_dev * top)
    owners = member * local + jnp.arange(local, dtype=jnp.int32)
    counts = (blocks[:, :, None] == owners[None, None, :]).astype(jnp.int32)
    ranks = jnp.cumsum(counts, axis=1) * counts - 1
    hits = (ranks[..., None] == jnp.arange(capacity, dtype=jnp.int32)).astype(jnp.int32)
    selector = hits.reshape(groups, tok_dev, top, local, capacity).sum(axis=2).astype(jnp.bfloat16)
    features = gathered.reshape(groups, tok_dev, gathered.shape[-1])
    return jnp.einsum(
        "ntec,ntd->necd", selector, features, preferred_element_type=jnp.float32
    ).astype(jnp.bfloat16)


def shards(tokens, expert_ids, gate_weights, norm_gain, w_gate, w_up, w_down):
    if fits(tokens, expert_ids, w_gate):
        return fused(tokens, expert_ids, gate_weights, norm_gain, w_gate, w_up, w_down)
    micro = tokens.shape[0]
    tok_dev = tokens.shape[1]
    width = tokens.shape[2]
    top = expert_ids.shape[-1]
    groups = lax.axis_size("expert")
    segments = lax.axis_size("segment")
    local = w_gate.shape[1]
    experts = local * groups
    capacity = 2 * tok_dev * top // experts
    segment_no = lax.axis_index("segment")
    member = lax.axis_index("expert")
    gain = norm_gain[0]
    weights = (w_gate[0], w_up[0], w_down[0])
    incoming = jnp.zeros((tok_dev, width), jnp.bfloat16)
    results = jnp.zeros((micro, tok_dev, width), jnp.bfloat16)
    total_ticks = micro + segments - 1
    for tick_no in range(total_ticks):
        offset = tick_no - segment_no
        micro_no = jnp.clip(offset, 0, micro - 1)
        fresh = tokens[min(tick_no, micro - 1)]
        current = jnp.where(segment_no == 0, fresh, incoming)
        routes = lax.dynamic_index_in_dim(expert_ids[0], micro_no, 0, keepdims=False)
        weighting = lax.dynamic_index_in_dim(gate_weights[0], micro_no, 0, keepdims=False)
        normed = norm_rows(current, gain)
        places = slot_index(routes, capacity, experts)
        gathered, all_routes = (
            lax.all_gather(normed, "expert", axis=0, tiled=True),
            lax.all_gather(routes, "expert", axis=0, tiled=True),
        )
        returned = serve_rows(
            pick_rows(gathered, all_routes, member, local, capacity, groups), weights
        )
        flat_back = returned.reshape(-1, width)
        picked = jnp.take(flat_back, places.reshape(-1), axis=0).reshape(tok_dev, top, width)
        mixed = (
            current.astype(jnp.float32)
            + jnp.sum(weighting[:, :, None] * picked.astype(jnp.float32), axis=1)
        ).astype(jnp.bfloat16)
        valid = (offset >= 0) & (offset < micro)
        updated = lax.dynamic_update_index_in_dim(results, mixed, micro_no, 0)
        results = jnp.where(valid, updated, results)
        if tick_no < total_ticks - 1:
            incoming = from_behind(mixed, "segment", 1)
    return results[None]


def solution(mesh):
    in_specs = (
        P(None, "expert", None),
        P("segment", None, "expert", None),
        P("segment", None, "expert", None),
        P("segment", None),
        P("segment", "expert", None, None),
        P("segment", "expert", None, None),
        P("segment", "expert", None, None),
    )
    out_specs = P("segment", None, "expert", None)
    return jax.shard_map(shards, mesh=mesh, in_specs=in_specs, out_specs=out_specs, check_vma=False)
```

```python
import functools

import jax
import jax.numpy as jnp
from jax import lax
from jax.experimental import pallas as pl
from jax.experimental.pallas import tpu as pltpu
from jax.sharding import PartitionSpec as P

PLANE = 4
CHUNKS = 4
LANES = 128
VMEM_BYTES = 60 * 1024 * 1024
MESH = pl.DeviceIdType.MESH


def vmem_need(micro, tok_dev, width, ff, groups):
    rows = tok_dev * groups
    weights = 3 * width * ff * 2
    features = 2 * micro * rows * width * 2
    landing = micro * (rows // PLANE) * width * 2 * 4 + micro * tok_dev * width * 2 * 6
    hidden = rows * ff * (8 + 2) + rows * LANES * 4
    return weights + features + landing + hidden


def relay_kernel(
    micro, segments, groups, tok_dev, width, ff, chunks,
    tok, ids, gw, gain, wg, wu, wd, out,
    xg, cur, outb, part, r1, r2, r3, zb, gb, wgv, wuv, wdv, acc, hid,
    wsem, zs, zr, xs, xr, fs, fr, r1s, r1r, r2s, r2r, r3s, r3r, cs, cr,
):
    depth = groups // PLANE
    wide = width // chunks
    bundle = depth * tok_dev
    half = bundle // 2
    seg = lax.axis_index("segment")
    me = lax.axis_index("expert")
    yx = me % PLANE
    z = me // PLANE
    xn = yx + 1 - 2 * (yx % 2)
    yn = yx + 2 - 4 * (yx // 2)
    across = PLANE - 1 - yx
    x_dev = z * PLANE + xn
    y_dev = z * PLANE + yn

    def rows(start, size):
        return pl.ds(pl.multiple_of(start, 16), size)

    def peer(d):
        return (z + d) % depth

    own_rows = rows((yx * depth + z) * tok_dev, tok_dev)

    def bundle_rows(which):
        return rows(which * bundle, bundle)

    def first_rows(which):
        return rows(which * bundle, half)

    def last_rows(which):
        return rows(which * bundle + half, half)

    def send(src, dst, s, r, dev):
        return pltpu.make_async_remote_copy(
            src_ref=src, dst_ref=dst, send_sem=s, recv_sem=r, device_id=(seg, dev), device_id_type=MESH
        )

    def feature(m, c):
        return gb if c is None else xg.at[m, c]

    def slot(c):
        return chunks if c is None else c

    def z_copy(m, c, d):
        ref = feature(m, c).at[own_rows]
        return send(ref, ref, zs.at[m, slot(c), d - 1], zr.at[m, slot(c), d - 1], peer(d) * PLANE + yx)

    def xy_copy(m, c, a):
        ref = feature(m, c).at[bundle_rows(yx)]
        return send(ref, ref, xs.at[m, slot(c), a], xr.at[m, slot(c), a], (x_dev, y_dev)[a])

    def f_copy(m, c, a):
        ref = feature(m, c).at[(first_rows(xn), last_rows(yn))[a]]
        return send(ref, ref, fs.at[m, slot(c), a], fr.at[m, slot(c), a], (y_dev, x_dev)[a])

    def z_send(m, c):
        for d in range(1, depth):
            z_copy(m, c, d).start()

    def xy_send(m, c):
        for d in range(1, depth):
            z_copy(m, c, d).wait_recv()
        for a in range(2):
            xy_copy(m, c, a).start()

    def f_send(m, c):
        for a in range(2):
            xy_copy(m, c, a).wait_recv()
            f_copy(m, c, a).start()

    def f_wait(m, c):
        for a in range(2):
            f_copy(m, c, a).wait_recv()

    def r1_copy(m, c, a):
        ref = part.at[m, c, (first_rows(across), last_rows(across))[a]]
        return send(ref, r1.at[m, c, a], r1s.at[m, c, a], r1r.at[m, c, a], (y_dev, x_dev)[a])

    def r2_copy(m, c, a):
        ref = part.at[m, c, bundle_rows((xn, yn)[a])]
        return send(ref, r2.at[m, c, a], r2s.at[m, c, a], r2r.at[m, c, a], (x_dev, y_dev)[a])

    def r3_copy(m, c, d):
        ref = zb.at[m, c, rows(peer(d) * tok_dev, tok_dev)]
        return send(ref, r3.at[m, c, d - 1], r3s.at[m, c, d - 1], r3r.at[m, c, d - 1], peer(d) * PLANE + yx)

    def relay_copy(m, c):
        return pltpu.make_async_remote_copy(
            src_ref=outb.at[m, c], dst_ref=cur.at[m, c], send_sem=cs.at[m, c], recv_sem=cr.at[m, c],
            device_id=(1 - seg, me), device_id_type=MESH,
        )

    f32 = jnp.float32

    def r2_send(m, c):
        for a in range(2):
            r1_copy(m, c, a).wait_recv()
            into = (first_rows(xn), last_rows(yn))[a]
            part[m, c, into] = (part[m, c, into].astype(f32) + r1[m, c, a].astype(f32)).astype(jnp.bfloat16)
            r2_copy(m, c, a).start()

    def r3_send(m, c):
        for a in range(2):
            r2_copy(m, c, a).wait_recv()
        total = part[m, c, bundle_rows(yx)].astype(f32) + r2[m, c, 0].astype(f32) + r2[m, c, 1].astype(f32)
        zb[m, c] = total.astype(jnp.bfloat16)
        for d in range(1, depth):
            r3_copy(m, c, d).start()

    def finish(m, c):
        for d in range(1, depth):
            r3_copy(m, c, d).wait_recv()
        inside = rows(z * tok_dev, tok_dev)
        total = part[m, c, own_rows].astype(f32) + r2[m, c, 0, inside].astype(f32) + r2[m, c, 1, inside].astype(f32)
        for d in range(1, depth):
            total = total + r3[m, c, d - 1].astype(f32)
        value = (cur[m, c].astype(f32) + total).astype(jnp.bfloat16)
        outb[m, c] = value
        out[m, :, pl.ds(pl.multiple_of(c * wide, LANES), wide)] = value

        @pl.when(seg == 0)
        def _():
            relay_copy(m, c).start()

    def weight_copy(which, c):
        src = (
            wg.at[rows(c * wide, wide)], wu.at[rows(c * wide, wide)],
            wd.at[:, pl.ds(pl.multiple_of(c * wide, LANES), wide)],
        )[which]
        return pltpu.make_async_copy(src, (wgv, wuv, wdv)[which].at[c], wsem.at[which, c])

    def up_chunk(m, c):
        f_wait(m, c)

        @pl.when(m == 0)
        def _():
            weight_copy(0, c).wait()
            weight_copy(1, c).wait()

        x = xg[m, c]
        gate = jnp.dot(x, wgv[c], preferred_element_type=f32)
        up = jnp.dot(x, wuv[c], preferred_element_type=f32)

        @pl.when(c == 0)
        def _():
            acc[0] = gate
            acc[1] = up

        @pl.when(c > 0)
        def _():
            acc[0] += gate
            acc[1] += up

    experts = groups

    def down_chunk(m, c):
        @pl.when(m == 0)
        def _():
            weight_copy(2, c).wait()

        lane = lax.broadcasted_iota(jnp.int32, (groups * tok_dev, LANES), 1)
        gate = jnp.sum(jnp.where(lane == m * experts + me, gb[...], 0.0), axis=1, keepdims=True)
        value = jnp.dot(hid[...], wdv[c], preferred_element_type=f32)
        part[m, c] = (value * gate).astype(jnp.bfloat16)
        for a in range(2):
            r1_copy(m, c, a).start()

    def take_in(m):
        @pl.when(seg == 0)
        def _():
            for c in range(chunks):
                cur[m, c] = tok[m, :, c * wide:(c + 1) * wide]

        @pl.when(seg > 0)
        def _():
            for c in range(chunks):
                relay_copy(m, c).wait_recv()

        square = jnp.zeros((tok_dev, 1), f32)
        for c in range(chunks):
            value = cur[m, c].astype(f32)
            square = square + jnp.sum(value * value, axis=1, keepdims=True)
        scale = lax.rsqrt(square / width + 1e-6)
        for c in range(chunks):
            value = cur[m, c].astype(f32) * scale * gain[:, c * wide:(c + 1) * wide]
            xg[m, c, own_rows] = value.astype(jnp.bfloat16)
            z_send(m, c)

    def hidden():
        gate = acc[0]
        hid[...] = (gate * jax.nn.sigmoid(gate) * acc[1]).astype(jnp.bfloat16)

    barrier = pltpu.get_barrier_semaphore()
    partners = [(seg, peer(d) * PLANE + yx) for d in range(1, depth)]
    partners += [(seg, x_dev), (seg, y_dev), (1 - seg, me)]
    for partner in partners:
        pl.semaphore_signal(barrier, inc=1, device_id=partner, device_id_type=MESH)
    for c in range(chunks):
        weight_copy(0, c).start()
        weight_copy(1, c).start()
    for c in range(chunks):
        weight_copy(2, c).start()

    row = lax.broadcasted_iota(jnp.int32, (LANES, tok_dev), 0)
    gates = jnp.zeros((LANES, tok_dev), f32)
    for m in range(micro):
        for k in range(ids.shape[1]):
            hit = row == ids[m, k:k + 1] + m * experts
            gates = gates + jnp.where(hit, gw[m, k:k + 1], 0.0)
    gb[own_rows] = gates.T
    pl.semaphore_wait(barrier, len(partners))

    take_in(0)
    z_send(0, None)

    late = 5 * seg
    plan = (
        (r3_send, 0, 12), (r3_send, 1, 19 + late), (r2_send, 0, 10), (r2_send, 1, 17 + late),
        (xy_send, 0, 0), (xy_send, 1, 5 + late), (f_send, 0, 2), (f_send, 1, 7 + late),
        (finish, 0, 14), (finish, 1, 21 + late), (up_chunk, 0, 4), (up_chunk, 1, 11 + late),
        (down_chunk, 0, 8), (down_chunk, 1, 15 + late),
    )

    def step(s, carry):
        @pl.when(s == 5 + late)
        def _():
            take_in(1)

        @pl.when(s == 4)
        def _():
            xy_send(0, None)

        @pl.when(s == 6)
        def _():
            f_send(0, None)

        @pl.when(s == 8)
        def _():
            f_wait(0, None)
            hidden()

        @pl.when(s == 15 + late)
        def _():
            hidden()

        for action, m, first in plan:
            @pl.when((s >= first) & (s < first + chunks))
            def _(action=action, m=m, first=first):
                action(m, s - first)

        return carry

    lax.fori_loop(0, 21 + chunks + late, step, 0)

    def sent(m, c, with_return):
        for d in range(1, depth):
            z_copy(m, c, d).wait_send()
        for a in range(2):
            xy_copy(m, c, a).wait_send()
            f_copy(m, c, a).wait_send()
        if with_return:
            for a in range(2):
                r1_copy(m, c, a).wait_send()
                r2_copy(m, c, a).wait_send()
            for d in range(1, depth):
                r3_copy(m, c, d).wait_send()

            @pl.when(seg == 0)
            def _():
                relay_copy(m, c).wait_send()

    def drain(i, carry):
        sent(i // chunks, i % chunks, True)
        return carry

    lax.fori_loop(0, micro * chunks, drain, 0)
    sent(0, None, False)


def fused(tokens, expert_ids, gate_weights, norm_gain, w_gate, w_up, w_down):
    micro, tok_dev, width = tokens.shape
    ff = w_gate.shape[-1]
    groups = lax.axis_size("expert")
    segments = lax.axis_size("segment")
    depth = groups // PLANE
    rows = groups * tok_dev
    bundle = depth * tok_dev
    chunks = CHUNKS
    wide = width // chunks
    bf16 = jnp.bfloat16
    dma = pltpu.SemaphoreType.DMA
    vmem = pl.BlockSpec(memory_space=pltpu.VMEM)
    hbm = pl.BlockSpec(memory_space=pl.ANY)
    scratch = [
        pltpu.VMEM((micro, chunks, rows, wide), bf16),
        pltpu.VMEM((micro, chunks, tok_dev, wide), bf16),
        pltpu.VMEM((micro, chunks, tok_dev, wide), bf16),
        pltpu.VMEM((micro, chunks, rows, wide), bf16),
        pltpu.VMEM((micro, chunks, 2, bundle // 2, wide), bf16),
        pltpu.VMEM((micro, chunks, 2, bundle, wide), bf16),
        pltpu.VMEM((micro, chunks, depth - 1, tok_dev, wide), bf16),
        pltpu.VMEM((micro, chunks, bundle, wide), bf16),
        pltpu.VMEM((rows, LANES), jnp.float32),
        pltpu.VMEM((chunks, wide, ff), bf16),
        pltpu.VMEM((chunks, wide, ff), bf16),
        pltpu.VMEM((chunks, ff, wide), bf16),
        pltpu.VMEM((2, rows, ff), jnp.float32),
        pltpu.VMEM((rows, ff), bf16),
        dma((3, chunks)),
    ]
    for count, kinds in ((chunks + 1, (depth - 1, 2, 2)), (chunks, (2, 2, depth - 1))):
        for kind in kinds:
            scratch += [dma((micro, count, kind))] * 2
    scratch += [dma((micro, chunks))] * 2
    result = pl.pallas_call(
        functools.partial(relay_kernel, micro, segments, groups, tok_dev, width, ff, chunks),
        out_shape=jax.ShapeDtypeStruct((micro, tok_dev, width), bf16),
        in_specs=[vmem, vmem, vmem, vmem, hbm, hbm, hbm],
        out_specs=vmem,
        scratch_shapes=scratch,
        compiler_params=pltpu.CompilerParams(
            collective_id=0, has_side_effects=True, vmem_limit_bytes=VMEM_BYTES
        ),
        cost_estimate=pl.CostEstimate(
            flops=micro * 6 * rows * width * ff, bytes_accessed=3 * width * ff * 2, transcendentals=micro * rows * ff
        ),
    )(tokens, jnp.swapaxes(expert_ids[0], 1, 2), jnp.swapaxes(gate_weights[0], 1, 2), norm_gain, w_gate[0, 0], w_up[0, 0], w_down[0, 0])
    return result[None]


def fits(tokens, expert_ids, w_gate):
    micro, tok_dev, width = tokens.shape
    groups = lax.axis_size("expert")
    return (
        lax.axis_size("segment") == 2
        and w_gate.shape[1] == 1
        and groups % PLANE == 0
        and groups > PLANE
        and (groups // PLANE) % 2 == 0
        and tok_dev % 16 == 0
        and width % (CHUNKS * LANES) == 0
        and micro * groups <= LANES
        and vmem_need(micro, tok_dev, width, w_gate.shape[3], groups) < VMEM_BYTES * 4 // 5
    )


def from_behind(value, axis, steps):
    count = lax.axis_size(axis)
    initial, last = (max(0, -steps), min(count, count - steps))
    return lax.ppermute(value, axis, [(source, source + steps) for source in range(initial, last)])


def norm_rows(current, gain):
    values = current.astype(jnp.float32)
    scaled = values * lax.rsqrt(jnp.mean(values * values, axis=-1, keepdims=True) + 1e-06)
    return (scaled * gain).astype(jnp.bfloat16)


def slot_index(routes, capacity, experts):
    flat = routes.reshape(-1)
    onehot = (flat[:, None] == jnp.arange(experts, dtype=jnp.int32)[None, :]).astype(jnp.int32)
    ranks = jnp.sum(jnp.cumsum(onehot, axis=0) * onehot, axis=1) - 1
    return (flat * capacity + ranks).reshape(routes.shape)


def expert_rows(received, weights):
    gate_all, up_all, down_all = weights
    row_block = received[:, 0].reshape(-1, received.shape[-1])
    gate_part = jnp.dot(row_block, gate_all[0], preferred_element_type=jnp.float32)
    up_part = jnp.dot(row_block, up_all[0], preferred_element_type=jnp.float32)
    hidden = (jax.nn.silu(gate_part) * up_part).astype(jnp.bfloat16)
    result = jnp.dot(hidden, down_all[0], preferred_element_type=jnp.float32).astype(jnp.bfloat16)
    outputs = [result.reshape(received.shape[0], received.shape[2], received.shape[3])]
    return jnp.stack(outputs, axis=1)


def serve_rows(received, weights):
    return lax.all_to_all(
        expert_rows(received, weights), "expert", split_axis=0, concat_axis=0, tiled=True
    )


def pick_rows(gathered, all_routes, member, local, capacity, groups):
    tok_dev = all_routes.shape[0] // groups
    top = all_routes.shape[1]
    blocks = all_routes.reshape(groups, tok_dev * top)
    owners = member * local + jnp.arange(local, dtype=jnp.int32)
    counts = (blocks[:, :, None] == owners[None, None, :]).astype(jnp.int32)
    ranks = jnp.cumsum(counts, axis=1) * counts - 1
    hits = (ranks[..., None] == jnp.arange(capacity, dtype=jnp.int32)).astype(jnp.int32)
    selector = hits.reshape(groups, tok_dev, top, local, capacity).sum(axis=2).astype(jnp.bfloat16)
    features = gathered.reshape(groups, tok_dev, gathered.shape[-1])
    return jnp.einsum(
        "ntec,ntd->necd", selector, features, preferred_element_type=jnp.float32
    ).astype(jnp.bfloat16)


def shards(tokens, expert_ids, gate_weights, norm_gain, w_gate, w_up, w_down):
    if fits(tokens, expert_ids, w_gate):
        return fused(tokens, expert_ids, gate_weights, norm_gain, w_gate, w_up, w_down)
    micro = tokens.shape[0]
    tok_dev = tokens.shape[1]
    width = tokens.shape[2]
    top = expert_ids.shape[-1]
    groups = lax.axis_size("expert")
    segments = lax.axis_size("segment")
    local = w_gate.shape[1]
    experts = local * groups
    capacity = 2 * tok_dev * top // experts
    segment_no = lax.axis_index("segment")
    member = lax.axis_index("expert")
    gain = norm_gain[0]
    weights = (w_gate[0], w_up[0], w_down[0])
    incoming = jnp.zeros((tok_dev, width), jnp.bfloat16)
    results = jnp.zeros((micro, tok_dev, width), jnp.bfloat16)
    total_ticks = micro + segments - 1
    for tick_no in range(total_ticks):
        offset = tick_no - segment_no
        micro_no = jnp.clip(offset, 0, micro - 1)
        fresh = tokens[min(tick_no, micro - 1)]
        current = jnp.where(segment_no == 0, fresh, incoming)
        routes = lax.dynamic_index_in_dim(expert_ids[0], micro_no, 0, keepdims=False)
        weighting = lax.dynamic_index_in_dim(gate_weights[0], micro_no, 0, keepdims=False)
        normed = norm_rows(current, gain)
        places = slot_index(routes, capacity, experts)
        gathered, all_routes = (
            lax.all_gather(normed, "expert", axis=0, tiled=True),
            lax.all_gather(routes, "expert", axis=0, tiled=True),
        )
        returned = serve_rows(
            pick_rows(gathered, all_routes, member, local, capacity, groups), weights
        )
        flat_back = returned.reshape(-1, width)
        picked = jnp.take(flat_back, places.reshape(-1), axis=0).reshape(tok_dev, top, width)
        mixed = (
            current.astype(jnp.float32)
            + jnp.sum(weighting[:, :, None] * picked.astype(jnp.float32), axis=1)
        ).astype(jnp.bfloat16)
        valid = (offset >= 0) & (offset < micro)
        updated = lax.dynamic_update_index_in_dim(results, mixed, micro_no, 0)
        results = jnp.where(valid, updated, results)
        if tick_no < total_ticks - 1:
            incoming = from_behind(mixed, "segment", 1)
    return results[None]


def solution(mesh):
    in_specs = (
        P(None, "expert", None),
        P("segment", None, "expert", None),
        P("segment", None, "expert", None),
        P("segment", None),
        P("segment", "expert", None, None),
        P("segment", "expert", None, None),
        P("segment", "expert", None, None),
    )
    out_specs = P("segment", None, "expert", None)
    return jax.shard_map(shards, mesh=mesh, in_specs=in_specs, out_specs=out_specs, check_vma=False)
```

```python
import functools

import jax
import jax.numpy as jnp
from jax import lax
from jax.experimental import pallas as pl
from jax.experimental.pallas import tpu as pltpu
from jax.sharding import PartitionSpec as P

PLANE = 4
CHUNKS = 4
LANES = 128
VMEM_BYTES = 60 * 1024 * 1024
MESH = pl.DeviceIdType.MESH


def vmem_need(micro, tok_dev, width, ff, groups):
    rows = tok_dev * groups
    weights = 3 * width * ff * 2
    features = 2 * micro * rows * width * 2
    landing = micro * (rows // PLANE) * width * 2 * 4 + micro * tok_dev * width * 2 * 6
    hidden = rows * ff * (8 + 2) + rows * LANES * 4
    return weights + features + landing + hidden


def relay_kernel(
    micro, segments, groups, tok_dev, width, ff, chunks,
    tok, ids, gw, gain, wg, wu, wd, out,
    xg, cur, outb, part, r1, r2, r3, zb, gb, wgv, wuv, wdv, acc, hid,
    wsem, zs, zr, xs, xr, fs, fr, r1s, r1r, r2s, r2r, r3s, r3r, cs, cr,
):
    depth = groups // PLANE
    wide = width // chunks
    bundle = depth * tok_dev
    half = bundle // 2
    seg = lax.axis_index("segment")
    me = lax.axis_index("expert")
    yx = me % PLANE
    z = me // PLANE
    xn = yx + 1 - 2 * (yx % 2)
    yn = yx + 2 - 4 * (yx // 2)
    across = PLANE - 1 - yx
    x_dev = z * PLANE + xn
    y_dev = z * PLANE + yn

    def rows(start, size):
        return pl.ds(pl.multiple_of(start, 16), size)

    def peer(d):
        return (z + d) % depth

    own_rows = rows((yx * depth + z) * tok_dev, tok_dev)

    def bundle_rows(which):
        return rows(which * bundle, bundle)

    def first_rows(which):
        return rows(which * bundle, half)

    def last_rows(which):
        return rows(which * bundle + half, half)

    def send(src, dst, s, r, dev):
        return pltpu.make_async_remote_copy(
            src_ref=src, dst_ref=dst, send_sem=s, recv_sem=r, device_id=(seg, dev), device_id_type=MESH
        )

    def feature(m, c):
        return gb if c is None else xg.at[m, c]

    def slot(c):
        return chunks if c is None else c

    def z_copy(m, c, d):
        ref = feature(m, c).at[own_rows]
        return send(ref, ref, zs.at[m, slot(c), d - 1], zr.at[m, slot(c), d - 1], peer(d) * PLANE + yx)

    def xy_copy(m, c, a):
        ref = feature(m, c).at[bundle_rows(yx)]
        return send(ref, ref, xs.at[m, slot(c), a], xr.at[m, slot(c), a], (x_dev, y_dev)[a])

    def f_copy(m, c, a):
        ref = feature(m, c).at[(first_rows(xn), last_rows(yn))[a]]
        return send(ref, ref, fs.at[m, slot(c), a], fr.at[m, slot(c), a], (y_dev, x_dev)[a])

    def z_send(m, c):
        for d in range(1, depth):
            z_copy(m, c, d).start()

    def xy_send(m, c):
        for d in range(1, depth):
            z_copy(m, c, d).wait_recv()
        for a in range(2):
            xy_copy(m, c, a).start()

    def f_send(m, c):
        for a in range(2):
            xy_copy(m, c, a).wait_recv()
            f_copy(m, c, a).start()

    def f_wait(m, c):
        for a in range(2):
            f_copy(m, c, a).wait_recv()

    def r1_copy(m, c, a):
        ref = part.at[m, c, (first_rows(across), last_rows(across))[a]]
        return send(ref, r1.at[m, c, a], r1s.at[m, c, a], r1r.at[m, c, a], (y_dev, x_dev)[a])

    def r2_copy(m, c, a):
        ref = part.at[m, c, bundle_rows((xn, yn)[a])]
        return send(ref, r2.at[m, c, a], r2s.at[m, c, a], r2r.at[m, c, a], (x_dev, y_dev)[a])

    def r3_copy(m, c, d):
        ref = zb.at[m, c, rows(peer(d) * tok_dev, tok_dev)]
        return send(ref, r3.at[m, c, d - 1], r3s.at[m, c, d - 1], r3r.at[m, c, d - 1], peer(d) * PLANE + yx)

    def relay_copy(m, c):
        return pltpu.make_async_remote_copy(
            src_ref=outb.at[m, c], dst_ref=cur.at[m, c], send_sem=cs.at[m, c], recv_sem=cr.at[m, c],
            device_id=(1 - seg, me), device_id_type=MESH,
        )

    f32 = jnp.float32

    def r2_send(m, c):
        for a in range(2):
            r1_copy(m, c, a).wait_recv()
            into = (first_rows(xn), last_rows(yn))[a]
            part[m, c, into] = (part[m, c, into].astype(f32) + r1[m, c, a].astype(f32)).astype(jnp.bfloat16)
            r2_copy(m, c, a).start()

    def r3_send(m, c):
        for a in range(2):
            r2_copy(m, c, a).wait_recv()
        total = part[m, c, bundle_rows(yx)].astype(f32) + r2[m, c, 0].astype(f32) + r2[m, c, 1].astype(f32)
        zb[m, c] = total.astype(jnp.bfloat16)
        for d in range(1, depth):
            r3_copy(m, c, d).start()

    def finish(m, c):
        for d in range(1, depth):
            r3_copy(m, c, d).wait_recv()
        inside = rows(z * tok_dev, tok_dev)
        total = part[m, c, own_rows].astype(f32) + r2[m, c, 0, inside].astype(f32) + r2[m, c, 1, inside].astype(f32)
        for d in range(1, depth):
            total = total + r3[m, c, d - 1].astype(f32)
        value = (cur[m, c].astype(f32) + total).astype(jnp.bfloat16)
        outb[m, c] = value
        out[m, :, pl.ds(pl.multiple_of(c * wide, LANES), wide)] = value

        @pl.when(seg == 0)
        def _():
            relay_copy(m, c).start()

    def weight_copy(which, c):
        src = (
            wg.at[rows(c * wide, wide)], wu.at[rows(c * wide, wide)],
            wd.at[:, pl.ds(pl.multiple_of(c * wide, LANES), wide)],
        )[which]
        return pltpu.make_async_copy(src, (wgv, wuv, wdv)[which].at[c], wsem.at[which, c])

    def up_chunk(m, c):
        f_wait(m, c)

        @pl.when(m == 0)
        def _():
            weight_copy(0, c).wait()
            weight_copy(1, c).wait()

        x = xg[m, c]
        gate = jnp.dot(x, wgv[c], preferred_element_type=f32)
        up = jnp.dot(x, wuv[c], preferred_element_type=f32)

        @pl.when(c == 0)
        def _():
            acc[0] = gate
            acc[1] = up

        @pl.when(c > 0)
        def _():
            acc[0] += gate
            acc[1] += up

    experts = groups

    def down_chunk(m, c):
        @pl.when(m == 0)
        def _():
            weight_copy(2, c).wait()

        lane = lax.broadcasted_iota(jnp.int32, (groups * tok_dev, LANES), 1)
        gate = jnp.sum(jnp.where(lane == m * experts + me, gb[...], 0.0), axis=1, keepdims=True)
        value = jnp.dot(hid[...], wdv[c], preferred_element_type=f32)
        part[m, c] = (value * gate).astype(jnp.bfloat16)
        for a in range(2):
            r1_copy(m, c, a).start()

    def take_in(m):
        @pl.when(seg == 0)
        def _():
            for c in range(chunks):
                cur[m, c] = tok[m, :, c * wide:(c + 1) * wide]

        @pl.when(seg > 0)
        def _():
            for c in range(chunks):
                relay_copy(m, c).wait_recv()

        square = jnp.zeros((tok_dev, 1), f32)
        for c in range(chunks):
            value = cur[m, c].astype(f32)
            square = square + jnp.sum(value * value, axis=1, keepdims=True)
        scale = lax.rsqrt(square / width + 1e-6)
        for c in range(chunks):
            value = cur[m, c].astype(f32) * scale * gain[:, c * wide:(c + 1) * wide]
            xg[m, c, own_rows] = value.astype(jnp.bfloat16)
            z_send(m, c)

    def hidden():
        gate = acc[0]
        hid[...] = (gate * jax.nn.sigmoid(gate) * acc[1]).astype(jnp.bfloat16)

    barrier = pltpu.get_barrier_semaphore()
    partners = [(seg, peer(d) * PLANE + yx) for d in range(1, depth)]
    partners += [(seg, x_dev), (seg, y_dev), (1 - seg, me)]
    for partner in partners:
        pl.semaphore_signal(barrier, inc=1, device_id=partner, device_id_type=MESH)
    for c in range(chunks):
        weight_copy(0, c).start()
        weight_copy(1, c).start()
    for c in range(chunks):
        weight_copy(2, c).start()

    row = lax.broadcasted_iota(jnp.int32, (LANES, tok_dev), 0)
    gates = jnp.zeros((LANES, tok_dev), f32)
    for m in range(micro):
        for k in range(ids.shape[1]):
            hit = row == ids[m, k:k + 1] + m * experts
            gates = gates + jnp.where(hit, gw[m, k:k + 1], 0.0)
    gb[own_rows] = gates.T
    pl.semaphore_wait(barrier, len(partners))

    take_in(0)
    z_send(0, None)

    def at(first, relayed):
        return first + (relayed - first) * seg

    n = chunks
    take_at = at(n - 2, 2 * n + 9)
    gates_at = n
    down_0 = n + 4
    down_1 = at(3 * n + 4, 3 * n + 14)
    fin_1 = at(3 * n + 12, 3 * n + 20)
    plan = (
        (r3_send, 0, n + 9), (r3_send, 1, at(3 * n + 9, 3 * n + 18)),
        (r2_send, 0, n + 6), (r2_send, 1, at(3 * n + 6, 3 * n + 16)),
        (xy_send, 0, 0), (xy_send, 1, at(n + 2, 2 * n + 10)),
        (f_send, 0, 2), (f_send, 1, at(n + 5, 2 * n + 12)),
        (finish, 0, n + 12), (finish, 1, fin_1),
        (up_chunk, 0, 4), (up_chunk, 1, at(2 * n + 4, 2 * n + 14)),
        (down_chunk, 0, down_0), (down_chunk, 1, down_1),
    )

    def step(s, carry):
        @pl.when(s == take_at)
        def _():
            take_in(1)

        @pl.when(s == gates_at)
        def _():
            xy_send(0, None)

        @pl.when(s == gates_at + 2)
        def _():
            f_send(0, None)

        @pl.when(s == down_0)
        def _():
            f_wait(0, None)
            hidden()

        @pl.when(s == down_1)
        def _():
            hidden()

        for action, m, first in plan:
            @pl.when((s >= first) & (s < first + chunks))
            def _(action=action, m=m, first=first):
                action(m, s - first)

        return carry

    lax.fori_loop(0, fin_1 + n, step, 0)

    def sent(m, c, with_return):
        for d in range(1, depth):
            z_copy(m, c, d).wait_send()
        for a in range(2):
            xy_copy(m, c, a).wait_send()
            f_copy(m, c, a).wait_send()
        if with_return:
            for a in range(2):
                r1_copy(m, c, a).wait_send()
                r2_copy(m, c, a).wait_send()
            for d in range(1, depth):
                r3_copy(m, c, d).wait_send()

            @pl.when(seg == 0)
            def _():
                relay_copy(m, c).wait_send()

    def drain(i, carry):
        sent(i // chunks, i % chunks, True)
        return carry

    lax.fori_loop(0, micro * chunks, drain, 0)
    sent(0, None, False)


def fused(tokens, expert_ids, gate_weights, norm_gain, w_gate, w_up, w_down):
    micro, tok_dev, width = tokens.shape
    ff = w_gate.shape[-1]
    groups = lax.axis_size("expert")
    segments = lax.axis_size("segment")
    depth = groups // PLANE
    rows = groups * tok_dev
    bundle = depth * tok_dev
    chunks = CHUNKS
    wide = width // chunks
    bf16 = jnp.bfloat16
    dma = pltpu.SemaphoreType.DMA
    vmem = pl.BlockSpec(memory_space=pltpu.VMEM)
    hbm = pl.BlockSpec(memory_space=pl.ANY)
    scratch = [
        pltpu.VMEM((micro, chunks, rows, wide), bf16),
        pltpu.VMEM((micro, chunks, tok_dev, wide), bf16),
        pltpu.VMEM((micro, chunks, tok_dev, wide), bf16),
        pltpu.VMEM((micro, chunks, rows, wide), bf16),
        pltpu.VMEM((micro, chunks, 2, bundle // 2, wide), bf16),
        pltpu.VMEM((micro, chunks, 2, bundle, wide), bf16),
        pltpu.VMEM((micro, chunks, depth - 1, tok_dev, wide), bf16),
        pltpu.VMEM((micro, chunks, bundle, wide), bf16),
        pltpu.VMEM((rows, LANES), jnp.float32),
        pltpu.VMEM((chunks, wide, ff), bf16),
        pltpu.VMEM((chunks, wide, ff), bf16),
        pltpu.VMEM((chunks, ff, wide), bf16),
        pltpu.VMEM((2, rows, ff), jnp.float32),
        pltpu.VMEM((rows, ff), bf16),
        dma((3, chunks)),
    ]
    for count, kinds in ((chunks + 1, (depth - 1, 2, 2)), (chunks, (2, 2, depth - 1))):
        for kind in kinds:
            scratch += [dma((micro, count, kind))] * 2
    scratch += [dma((micro, chunks))] * 2
    result = pl.pallas_call(
        functools.partial(relay_kernel, micro, segments, groups, tok_dev, width, ff, chunks),
        out_shape=jax.ShapeDtypeStruct((micro, tok_dev, width), bf16),
        in_specs=[vmem, vmem, vmem, vmem, hbm, hbm, hbm],
        out_specs=vmem,
        scratch_shapes=scratch,
        compiler_params=pltpu.CompilerParams(
            collective_id=0, has_side_effects=True, vmem_limit_bytes=VMEM_BYTES
        ),
        cost_estimate=pl.CostEstimate(
            flops=micro * 6 * rows * width * ff, bytes_accessed=3 * width * ff * 2, transcendentals=micro * rows * ff
        ),
    )(tokens, jnp.swapaxes(expert_ids[0], 1, 2), jnp.swapaxes(gate_weights[0], 1, 2), norm_gain, w_gate[0, 0], w_up[0, 0], w_down[0, 0])
    return result[None]


def fits(tokens, expert_ids, w_gate):
    micro, tok_dev, width = tokens.shape
    groups = lax.axis_size("expert")
    return (
        lax.axis_size("segment") == 2
        and w_gate.shape[1] == 1
        and groups % PLANE == 0
        and groups > PLANE
        and (groups // PLANE) % 2 == 0
        and tok_dev % 16 == 0
        and width % (CHUNKS * LANES) == 0
        and micro * groups <= LANES
        and vmem_need(micro, tok_dev, width, w_gate.shape[3], groups) < VMEM_BYTES * 4 // 5
    )


def from_behind(value, axis, steps):
    count = lax.axis_size(axis)
    initial, last = (max(0, -steps), min(count, count - steps))
    return lax.ppermute(value, axis, [(source, source + steps) for source in range(initial, last)])


def norm_rows(current, gain):
    values = current.astype(jnp.float32)
    scaled = values * lax.rsqrt(jnp.mean(values * values, axis=-1, keepdims=True) + 1e-06)
    return (scaled * gain).astype(jnp.bfloat16)


def slot_index(routes, capacity, experts):
    flat = routes.reshape(-1)
    onehot = (flat[:, None] == jnp.arange(experts, dtype=jnp.int32)[None, :]).astype(jnp.int32)
    ranks = jnp.sum(jnp.cumsum(onehot, axis=0) * onehot, axis=1) - 1
    return (flat * capacity + ranks).reshape(routes.shape)


def expert_rows(received, weights):
    gate_all, up_all, down_all = weights
    row_block = received[:, 0].reshape(-1, received.shape[-1])
    gate_part = jnp.dot(row_block, gate_all[0], preferred_element_type=jnp.float32)
    up_part = jnp.dot(row_block, up_all[0], preferred_element_type=jnp.float32)
    hidden = (jax.nn.silu(gate_part) * up_part).astype(jnp.bfloat16)
    result = jnp.dot(hidden, down_all[0], preferred_element_type=jnp.float32).astype(jnp.bfloat16)
    outputs = [result.reshape(received.shape[0], received.shape[2], received.shape[3])]
    return jnp.stack(outputs, axis=1)


def serve_rows(received, weights):
    return lax.all_to_all(
        expert_rows(received, weights), "expert", split_axis=0, concat_axis=0, tiled=True
    )


def pick_rows(gathered, all_routes, member, local, capacity, groups):
    tok_dev = all_routes.shape[0] // groups
    top = all_routes.shape[1]
    blocks = all_routes.reshape(groups, tok_dev * top)
    owners = member * local + jnp.arange(local, dtype=jnp.int32)
    counts = (blocks[:, :, None] == owners[None, None, :]).astype(jnp.int32)
    ranks = jnp.cumsum(counts, axis=1) * counts - 1
    hits = (ranks[..., None] == jnp.arange(capacity, dtype=jnp.int32)).astype(jnp.int32)
    selector = hits.reshape(groups, tok_dev, top, local, capacity).sum(axis=2).astype(jnp.bfloat16)
    features = gathered.reshape(groups, tok_dev, gathered.shape[-1])
    return jnp.einsum(
        "ntec,ntd->necd", selector, features, preferred_element_type=jnp.float32
    ).astype(jnp.bfloat16)


def shards(tokens, expert_ids, gate_weights, norm_gain, w_gate, w_up, w_down):
    if fits(tokens, expert_ids, w_gate):
        return fused(tokens, expert_ids, gate_weights, norm_gain, w_gate, w_up, w_down)
    micro = tokens.shape[0]
    tok_dev = tokens.shape[1]
    width = tokens.shape[2]
    top = expert_ids.shape[-1]
    groups = lax.axis_size("expert")
    segments = lax.axis_size("segment")
    local = w_gate.shape[1]
    experts = local * groups
    capacity = 2 * tok_dev * top // experts
    segment_no = lax.axis_index("segment")
    member = lax.axis_index("expert")
    gain = norm_gain[0]
    weights = (w_gate[0], w_up[0], w_down[0])
    incoming = jnp.zeros((tok_dev, width), jnp.bfloat16)
    results = jnp.zeros((micro, tok_dev, width), jnp.bfloat16)
    total_ticks = micro + segments - 1
    for tick_no in range(total_ticks):
        offset = tick_no - segment_no
        micro_no = jnp.clip(offset, 0, micro - 1)
        fresh = tokens[min(tick_no, micro - 1)]
        current = jnp.where(segment_no == 0, fresh, incoming)
        routes = lax.dynamic_index_in_dim(expert_ids[0], micro_no, 0, keepdims=False)
        weighting = lax.dynamic_index_in_dim(gate_weights[0], micro_no, 0, keepdims=False)
        normed = norm_rows(current, gain)
        places = slot_index(routes, capacity, experts)
        gathered, all_routes = (
            lax.all_gather(normed, "expert", axis=0, tiled=True),
            lax.all_gather(routes, "expert", axis=0, tiled=True),
        )
        returned = serve_rows(
            pick_rows(gathered, all_routes, member, local, capacity, groups), weights
        )
        flat_back = returned.reshape(-1, width)
        picked = jnp.take(flat_back, places.reshape(-1), axis=0).reshape(tok_dev, top, width)
        mixed = (
            current.astype(jnp.float32)
            + jnp.sum(weighting[:, :, None] * picked.astype(jnp.float32), axis=1)
        ).astype(jnp.bfloat16)
        valid = (offset >= 0) & (offset < micro)
        updated = lax.dynamic_update_index_in_dim(results, mixed, micro_no, 0)
        results = jnp.where(valid, updated, results)
        if tick_no < total_ticks - 1:
            incoming = from_behind(mixed, "segment", 1)
    return results[None]


def solution(mesh):
    in_specs = (
        P(None, "expert", None),
        P("segment", None, "expert", None),
        P("segment", None, "expert", None),
        P("segment", None),
        P("segment", "expert", None, None),
        P("segment", "expert", None, None),
        P("segment", "expert", None, None),
    )
    out_specs = P("segment", None, "expert", None)
    return jax.shard_map(shards, mesh=mesh, in_specs=in_specs, out_specs=out_specs, check_vma=False)
```

```python
import functools

import jax
import jax.numpy as jnp
from jax import lax
from jax.experimental import pallas as pl
from jax.experimental.pallas import tpu as pltpu
from jax.sharding import PartitionSpec as P

PLANE = 4
CHUNKS = 4
LANES = 128
VMEM_BYTES = 60 * 1024 * 1024
MESH = pl.DeviceIdType.MESH


def vmem_need(micro, tok_dev, width, ff, groups):
    rows = tok_dev * groups
    weights = 3 * width * ff * 2
    features = 2 * micro * rows * width * 2
    landing = micro * (rows // PLANE) * width * 2 * 4 + micro * tok_dev * width * 2 * 6
    hidden = rows * ff * (8 + 2) + rows * LANES * 4
    return weights + features + landing + hidden


def relay_kernel(
    micro, segments, groups, tok_dev, width, ff, chunks,
    tok, ids, gw, gain, wg, wu, wd, out,
    xg, cur, outb, part, r1, r2, r3, zb, gb, wgv, wuv, wdv, acc, hid,
    wsem, zs, zr, xs, xr, fs, fr, r1s, r1r, r2s, r2r, r3s, r3r, cs, cr,
):
    depth = groups // PLANE
    wide = width // chunks
    bundle = depth * tok_dev
    half = bundle // 2
    seg = lax.axis_index("segment")
    me = lax.axis_index("expert")
    yx = me % PLANE
    z = me // PLANE
    xn = yx + 1 - 2 * (yx % 2)
    yn = yx + 2 - 4 * (yx // 2)
    across = PLANE - 1 - yx
    x_dev = z * PLANE + xn
    y_dev = z * PLANE + yn

    def rows(start, size):
        return pl.ds(pl.multiple_of(start, 16), size)

    def peer(d):
        return (z + d) % depth

    own_rows = rows((yx * depth + z) * tok_dev, tok_dev)

    def bundle_rows(which):
        return rows(which * bundle, bundle)

    def first_rows(which):
        return rows(which * bundle, half)

    def last_rows(which):
        return rows(which * bundle + half, half)

    def send(src, dst, s, r, dev):
        return pltpu.make_async_remote_copy(
            src_ref=src, dst_ref=dst, send_sem=s, recv_sem=r, device_id=(seg, dev), device_id_type=MESH
        )

    def feature(m, c):
        return gb if c is None else xg.at[m, c]

    def slot(c):
        return chunks if c is None else c

    def z_copy(m, c, d):
        ref = feature(m, c).at[own_rows]
        return send(ref, ref, zs.at[m, slot(c), d - 1], zr.at[m, slot(c), d - 1], peer(d) * PLANE + yx)

    def xy_copy(m, c, a):
        ref = feature(m, c).at[bundle_rows(yx)]
        return send(ref, ref, xs.at[m, slot(c), a], xr.at[m, slot(c), a], (x_dev, y_dev)[a])

    def f_copy(m, c, a):
        ref = feature(m, c).at[(first_rows(xn), last_rows(yn))[a]]
        return send(ref, ref, fs.at[m, slot(c), a], fr.at[m, slot(c), a], (y_dev, x_dev)[a])

    def z_send(m, c):
        for d in range(1, depth):
            z_copy(m, c, d).start()

    def xy_send(m, c):
        for d in range(1, depth):
            z_copy(m, c, d).wait_recv()
        for a in range(2):
            xy_copy(m, c, a).start()

    def f_send(m, c):
        for a in range(2):
            xy_copy(m, c, a).wait_recv()
            f_copy(m, c, a).start()

    def f_wait(m, c):
        for a in range(2):
            f_copy(m, c, a).wait_recv()

    def r1_copy(m, c, a):
        ref = part.at[m, c, (first_rows(across), last_rows(across))[a]]
        return send(ref, r1.at[m, c, a], r1s.at[m, c, a], r1r.at[m, c, a], (y_dev, x_dev)[a])

    def r2_copy(m, c, a):
        ref = part.at[m, c, bundle_rows((xn, yn)[a])]
        return send(ref, r2.at[m, c, a], r2s.at[m, c, a], r2r.at[m, c, a], (x_dev, y_dev)[a])

    def r3_copy(m, c, d):
        ref = zb.at[m, c, rows(peer(d) * tok_dev, tok_dev)]
        return send(ref, r3.at[m, c, d - 1], r3s.at[m, c, d - 1], r3r.at[m, c, d - 1], peer(d) * PLANE + yx)

    def relay_copy(m, c):
        return pltpu.make_async_remote_copy(
            src_ref=outb.at[m, c], dst_ref=cur.at[m, c], send_sem=cs.at[m, c], recv_sem=cr.at[m, c],
            device_id=(1 - seg, me), device_id_type=MESH,
        )

    f32 = jnp.float32

    def r2_send(m, c):
        for a in range(2):
            r1_copy(m, c, a).wait_recv()
            into = (first_rows(xn), last_rows(yn))[a]
            part[m, c, into] = (part[m, c, into].astype(f32) + r1[m, c, a].astype(f32)).astype(jnp.bfloat16)
            r2_copy(m, c, a).start()

    def r3_send(m, c):
        for a in range(2):
            r2_copy(m, c, a).wait_recv()
        total = part[m, c, bundle_rows(yx)].astype(f32) + r2[m, c, 0].astype(f32) + r2[m, c, 1].astype(f32)
        zb[m, c] = total.astype(jnp.bfloat16)
        for d in range(1, depth):
            r3_copy(m, c, d).start()

    def gather_sent(m, c):
        for d in range(1, depth):
            z_copy(m, c, d).wait_send()
        for a in range(2):
            xy_copy(m, c, a).wait_send()
            f_copy(m, c, a).wait_send()

    def finish(m, c):
        gather_sent(m, c)
        for a in range(2):
            r1_copy(m, c, a).wait_send()
            r2_copy(m, c, a).wait_send()
        for d in range(1, depth):
            r3_copy(m, c, d).wait_recv()
        inside = rows(z * tok_dev, tok_dev)
        total = part[m, c, own_rows].astype(f32) + r2[m, c, 0, inside].astype(f32) + r2[m, c, 1, inside].astype(f32)
        for d in range(1, depth):
            total = total + r3[m, c, d - 1].astype(f32)
        value = (cur[m, c].astype(f32) + total).astype(jnp.bfloat16)
        outb[m, c] = value
        out[m, :, pl.ds(pl.multiple_of(c * wide, LANES), wide)] = value

        @pl.when(seg == 0)
        def _():
            relay_copy(m, c).start()

    def weight_copy(which, c):
        src = (
            wg.at[rows(c * wide, wide)], wu.at[rows(c * wide, wide)],
            wd.at[:, pl.ds(pl.multiple_of(c * wide, LANES), wide)],
        )[which]
        return pltpu.make_async_copy(src, (wgv, wuv, wdv)[which].at[c], wsem.at[which, c])

    def up_chunk(m, c):
        f_wait(m, c)

        @pl.when(m == 0)
        def _():
            weight_copy(0, c).wait()
            weight_copy(1, c).wait()

        x = xg[m, c]
        gate = jnp.dot(x, wgv[c], preferred_element_type=f32)
        up = jnp.dot(x, wuv[c], preferred_element_type=f32)

        @pl.when(c == 0)
        def _():
            acc[0] = gate
            acc[1] = up

        @pl.when(c > 0)
        def _():
            acc[0] += gate
            acc[1] += up

    experts = groups

    def down_chunk(m, c):
        @pl.when(m == 0)
        def _():
            weight_copy(2, c).wait()

        lane = lax.broadcasted_iota(jnp.int32, (groups * tok_dev, LANES), 1)
        gate = jnp.sum(jnp.where(lane == m * experts + me, gb[...], 0.0), axis=1, keepdims=True)
        value = jnp.dot(hid[...], wdv[c], preferred_element_type=f32)
        part[m, c] = (value * gate).astype(jnp.bfloat16)
        for a in range(2):
            r1_copy(m, c, a).start()

    def take_in(m):
        @pl.when(seg == 0)
        def _():
            for c in range(chunks):
                cur[m, c] = tok[m, :, c * wide:(c + 1) * wide]

        @pl.when(seg > 0)
        def _():
            for c in range(chunks):
                relay_copy(m, c).wait_recv()

        square = jnp.zeros((tok_dev, 1), f32)
        for c in range(chunks):
            value = cur[m, c].astype(f32)
            square = square + jnp.sum(value * value, axis=1, keepdims=True)
        scale = lax.rsqrt(square / width + 1e-6)
        for c in range(chunks):
            value = cur[m, c].astype(f32) * scale * gain[:, c * wide:(c + 1) * wide]
            xg[m, c, own_rows] = value.astype(jnp.bfloat16)
            z_send(m, c)

    def hidden():
        gate = acc[0]
        hid[...] = (gate * jax.nn.sigmoid(gate) * acc[1]).astype(jnp.bfloat16)

    barrier = pltpu.get_barrier_semaphore()
    partners = [(seg, peer(d) * PLANE + yx) for d in range(1, depth)]
    partners += [(seg, x_dev), (seg, y_dev), (1 - seg, me)]
    for partner in partners:
        pl.semaphore_signal(barrier, inc=1, device_id=partner, device_id_type=MESH)
    for c in range(chunks):
        weight_copy(0, c).start()
        weight_copy(1, c).start()
    for c in range(chunks):
        weight_copy(2, c).start()

    row = lax.broadcasted_iota(jnp.int32, (LANES, tok_dev), 0)
    gates = jnp.zeros((LANES, tok_dev), f32)
    for m in range(micro):
        for k in range(ids.shape[1]):
            hit = row == ids[m, k:k + 1] + m * experts
            gates = gates + jnp.where(hit, gw[m, k:k + 1], 0.0)
    gb[own_rows] = gates.T
    pl.semaphore_wait(barrier, len(partners))

    take_in(0)
    z_send(0, None)

    def at(first, relayed):
        return first + (relayed - first) * seg

    n = chunks
    take_at = at(n - 2, n + 8)
    gates_at = n
    down_0 = n + 4
    down_1 = at(3 * n + 4, 2 * n + 14)
    fin_1 = at(3 * n + 12, 2 * n + 20)
    plan = (
        (r3_send, 0, n + 9), (r3_send, 1, at(3 * n + 9, 2 * n + 18)),
        (r2_send, 0, n + 6), (r2_send, 1, at(3 * n + 6, 2 * n + 16)),
        (xy_send, 0, 0), (xy_send, 1, at(n + 2, n + 10)),
        (f_send, 0, 2), (f_send, 1, at(n + 5, n + 12)),
        (finish, 0, n + 12), (finish, 1, fin_1),
        (up_chunk, 0, 4), (up_chunk, 1, at(2 * n + 4, n + 14)),
        (down_chunk, 0, down_0), (down_chunk, 1, down_1),
    )

    def step(s, carry):
        @pl.when(s == take_at)
        def _():
            take_in(1)

        @pl.when(s == gates_at)
        def _():
            xy_send(0, None)

        @pl.when(s == gates_at + 2)
        def _():
            f_send(0, None)

        @pl.when(s == down_0)
        def _():
            f_wait(0, None)
            hidden()

        @pl.when(s == down_1)
        def _():
            hidden()

        for action, m, first in plan:
            @pl.when((s >= first) & (s < first + chunks))
            def _(action=action, m=m, first=first):
                action(m, s - first)

        return carry

    lax.fori_loop(0, fin_1 + n, step, 0)

    def drain(i, carry):
        m = i // chunks
        c = i % chunks
        for d in range(1, depth):
            r3_copy(m, c, d).wait_send()

        @pl.when(seg == 0)
        def _():
            relay_copy(m, c).wait_send()

        return carry

    lax.fori_loop(0, micro * chunks, drain, 0)
    gather_sent(0, None)


def fused(tokens, expert_ids, gate_weights, norm_gain, w_gate, w_up, w_down):
    micro, tok_dev, width = tokens.shape
    ff = w_gate.shape[-1]
    groups = lax.axis_size("expert")
    segments = lax.axis_size("segment")
    depth = groups // PLANE
    rows = groups * tok_dev
    bundle = depth * tok_dev
    chunks = CHUNKS
    wide = width // chunks
    bf16 = jnp.bfloat16
    dma = pltpu.SemaphoreType.DMA
    vmem = pl.BlockSpec(memory_space=pltpu.VMEM)
    hbm = pl.BlockSpec(memory_space=pl.ANY)
    scratch = [
        pltpu.VMEM((micro, chunks, rows, wide), bf16),
        pltpu.VMEM((micro, chunks, tok_dev, wide), bf16),
        pltpu.VMEM((micro, chunks, tok_dev, wide), bf16),
        pltpu.VMEM((micro, chunks, rows, wide), bf16),
        pltpu.VMEM((micro, chunks, 2, bundle // 2, wide), bf16),
        pltpu.VMEM((micro, chunks, 2, bundle, wide), bf16),
        pltpu.VMEM((micro, chunks, depth - 1, tok_dev, wide), bf16),
        pltpu.VMEM((micro, chunks, bundle, wide), bf16),
        pltpu.VMEM((rows, LANES), jnp.float32),
        pltpu.VMEM((chunks, wide, ff), bf16),
        pltpu.VMEM((chunks, wide, ff), bf16),
        pltpu.VMEM((chunks, ff, wide), bf16),
        pltpu.VMEM((2, rows, ff), jnp.float32),
        pltpu.VMEM((rows, ff), bf16),
        dma((3, chunks)),
    ]
    for count, kinds in ((chunks + 1, (depth - 1, 2, 2)), (chunks, (2, 2, depth - 1))):
        for kind in kinds:
            scratch += [dma((micro, count, kind))] * 2
    scratch += [dma((micro, chunks))] * 2
    result = pl.pallas_call(
        functools.partial(relay_kernel, micro, segments, groups, tok_dev, width, ff, chunks),
        out_shape=jax.ShapeDtypeStruct((micro, tok_dev, width), bf16),
        in_specs=[vmem, vmem, vmem, vmem, hbm, hbm, hbm],
        out_specs=vmem,
        scratch_shapes=scratch,
        compiler_params=pltpu.CompilerParams(
            collective_id=0, has_side_effects=True, vmem_limit_bytes=VMEM_BYTES
        ),
        cost_estimate=pl.CostEstimate(
            flops=micro * 6 * rows * width * ff, bytes_accessed=3 * width * ff * 2, transcendentals=micro * rows * ff
        ),
    )(tokens, jnp.swapaxes(expert_ids[0], 1, 2), jnp.swapaxes(gate_weights[0], 1, 2), norm_gain, w_gate[0, 0], w_up[0, 0], w_down[0, 0])
    return result[None]


def fits(tokens, expert_ids, w_gate):
    micro, tok_dev, width = tokens.shape
    groups = lax.axis_size("expert")
    return (
        lax.axis_size("segment") == 2
        and w_gate.shape[1] == 1
        and groups % PLANE == 0
        and groups > PLANE
        and (groups // PLANE) % 2 == 0
        and tok_dev % 16 == 0
        and width % (CHUNKS * LANES) == 0
        and micro * groups <= LANES
        and vmem_need(micro, tok_dev, width, w_gate.shape[3], groups) < VMEM_BYTES * 4 // 5
    )


def from_behind(value, axis, steps):
    count = lax.axis_size(axis)
    initial, last = (max(0, -steps), min(count, count - steps))
    return lax.ppermute(value, axis, [(source, source + steps) for source in range(initial, last)])


def norm_rows(current, gain):
    values = current.astype(jnp.float32)
    scaled = values * lax.rsqrt(jnp.mean(values * values, axis=-1, keepdims=True) + 1e-06)
    return (scaled * gain).astype(jnp.bfloat16)


def slot_index(routes, capacity, experts):
    flat = routes.reshape(-1)
    onehot = (flat[:, None] == jnp.arange(experts, dtype=jnp.int32)[None, :]).astype(jnp.int32)
    ranks = jnp.sum(jnp.cumsum(onehot, axis=0) * onehot, axis=1) - 1
    return (flat * capacity + ranks).reshape(routes.shape)


def expert_rows(received, weights):
    gate_all, up_all, down_all = weights
    row_block = received[:, 0].reshape(-1, received.shape[-1])
    gate_part = jnp.dot(row_block, gate_all[0], preferred_element_type=jnp.float32)
    up_part = jnp.dot(row_block, up_all[0], preferred_element_type=jnp.float32)
    hidden = (jax.nn.silu(gate_part) * up_part).astype(jnp.bfloat16)
    result = jnp.dot(hidden, down_all[0], preferred_element_type=jnp.float32).astype(jnp.bfloat16)
    outputs = [result.reshape(received.shape[0], received.shape[2], received.shape[3])]
    return jnp.stack(outputs, axis=1)


def serve_rows(received, weights):
    return lax.all_to_all(
        expert_rows(received, weights), "expert", split_axis=0, concat_axis=0, tiled=True
    )


def pick_rows(gathered, all_routes, member, local, capacity, groups):
    tok_dev = all_routes.shape[0] // groups
    top = all_routes.shape[1]
    blocks = all_routes.reshape(groups, tok_dev * top)
    owners = member * local + jnp.arange(local, dtype=jnp.int32)
    counts = (blocks[:, :, None] == owners[None, None, :]).astype(jnp.int32)
    ranks = jnp.cumsum(counts, axis=1) * counts - 1
    hits = (ranks[..., None] == jnp.arange(capacity, dtype=jnp.int32)).astype(jnp.int32)
    selector = hits.reshape(groups, tok_dev, top, local, capacity).sum(axis=2).astype(jnp.bfloat16)
    features = gathered.reshape(groups, tok_dev, gathered.shape[-1])
    return jnp.einsum(
        "ntec,ntd->necd", selector, features, preferred_element_type=jnp.float32
    ).astype(jnp.bfloat16)


def shards(tokens, expert_ids, gate_weights, norm_gain, w_gate, w_up, w_down):
    if fits(tokens, expert_ids, w_gate):
        return fused(tokens, expert_ids, gate_weights, norm_gain, w_gate, w_up, w_down)
    micro = tokens.shape[0]
    tok_dev = tokens.shape[1]
    width = tokens.shape[2]
    top = expert_ids.shape[-1]
    groups = lax.axis_size("expert")
    segments = lax.axis_size("segment")
    local = w_gate.shape[1]
    experts = local * groups
    capacity = 2 * tok_dev * top // experts
    segment_no = lax.axis_index("segment")
    member = lax.axis_index("expert")
    gain = norm_gain[0]
    weights = (w_gate[0], w_up[0], w_down[0])
    incoming = jnp.zeros((tok_dev, width), jnp.bfloat16)
    results = jnp.zeros((micro, tok_dev, width), jnp.bfloat16)
    total_ticks = micro + segments - 1
    for tick_no in range(total_ticks):
        offset = tick_no - segment_no
        micro_no = jnp.clip(offset, 0, micro - 1)
        fresh = tokens[min(tick_no, micro - 1)]
        current = jnp.where(segment_no == 0, fresh, incoming)
        routes = lax.dynamic_index_in_dim(expert_ids[0], micro_no, 0, keepdims=False)
        weighting = lax.dynamic_index_in_dim(gate_weights[0], micro_no, 0, keepdims=False)
        normed = norm_rows(current, gain)
        places = slot_index(routes, capacity, experts)
        gathered, all_routes = (
            lax.all_gather(normed, "expert", axis=0, tiled=True),
            lax.all_gather(routes, "expert", axis=0, tiled=True),
        )
        returned = serve_rows(
            pick_rows(gathered, all_routes, member, local, capacity, groups), weights
        )
        flat_back = returned.reshape(-1, width)
        picked = jnp.take(flat_back, places.reshape(-1), axis=0).reshape(tok_dev, top, width)
        mixed = (
            current.astype(jnp.float32)
            + jnp.sum(weighting[:, :, None] * picked.astype(jnp.float32), axis=1)
        ).astype(jnp.bfloat16)
        valid = (offset >= 0) & (offset < micro)
        updated = lax.dynamic_update_index_in_dim(results, mixed, micro_no, 0)
        results = jnp.where(valid, updated, results)
        if tick_no < total_ticks - 1:
            incoming = from_behind(mixed, "segment", 1)
    return results[None]


def solution(mesh):
    in_specs = (
        P(None, "expert", None),
        P("segment", None, "expert", None),
        P("segment", None, "expert", None),
        P("segment", None),
        P("segment", "expert", None, None),
        P("segment", "expert", None, None),
        P("segment", "expert", None, None),
    )
    out_specs = P("segment", None, "expert", None)
    return jax.shard_map(shards, mesh=mesh, in_specs=in_specs, out_specs=out_specs, check_vma=False)
```

```python
import functools

import jax
import jax.numpy as jnp
from jax import lax
from jax.experimental import pallas as pl
from jax.experimental.pallas import tpu as pltpu
from jax.sharding import PartitionSpec as P

PLANE = 4
CHUNKS = 8
LANES = 128
VMEM_BYTES = 60 * 1024 * 1024
MESH = pl.DeviceIdType.MESH


def vmem_need(micro, tok_dev, width, ff, groups):
    rows = tok_dev * groups
    weights = 3 * width * ff * 2
    features = 2 * micro * rows * width * 2
    landing = micro * (rows // PLANE) * width * 2 * 4 + micro * tok_dev * width * 2 * 6
    hidden = rows * ff * (8 + 2) + rows * LANES * 4
    return weights + features + landing + hidden


def relay_kernel(
    micro, segments, groups, tok_dev, width, ff, chunks,
    tok, ids, gw, gain, wg, wu, wd, out,
    xg, cur, outb, part, r1, r2, r3, zb, gb, wgv, wuv, wdv, acc, hid,
    wsem, zs, zr, xs, xr, fs, fr, r1s, r1r, r2s, r2r, r3s, r3r, cs, cr,
):
    depth = groups // PLANE
    wide = width // chunks
    bundle = depth * tok_dev
    half = bundle // 2
    seg = lax.axis_index("segment")
    me = lax.axis_index("expert")
    yx = me % PLANE
    z = me // PLANE
    xn = yx + 1 - 2 * (yx % 2)
    yn = yx + 2 - 4 * (yx // 2)
    across = PLANE - 1 - yx
    x_dev = z * PLANE + xn
    y_dev = z * PLANE + yn

    def rows(start, size):
        return pl.ds(pl.multiple_of(start, 16), size)

    def peer(d):
        return (z + d) % depth

    own_rows = rows((yx * depth + z) * tok_dev, tok_dev)

    def bundle_rows(which):
        return rows(which * bundle, bundle)

    def first_rows(which):
        return rows(which * bundle, half)

    def last_rows(which):
        return rows(which * bundle + half, half)

    def send(src, dst, s, r, dev):
        return pltpu.make_async_remote_copy(
            src_ref=src, dst_ref=dst, send_sem=s, recv_sem=r, device_id=(seg, dev), device_id_type=MESH
        )

    def feature(m, c):
        return gb if c is None else xg.at[m, c]

    def slot(c):
        return chunks if c is None else c

    def z_copy(m, c, d):
        ref = feature(m, c).at[own_rows]
        return send(ref, ref, zs.at[m, slot(c), d - 1], zr.at[m, slot(c), d - 1], peer(d) * PLANE + yx)

    def xy_copy(m, c, a):
        ref = feature(m, c).at[bundle_rows(yx)]
        return send(ref, ref, xs.at[m, slot(c), a], xr.at[m, slot(c), a], (x_dev, y_dev)[a])

    def f_copy(m, c, a):
        ref = feature(m, c).at[(first_rows(xn), last_rows(yn))[a]]
        return send(ref, ref, fs.at[m, slot(c), a], fr.at[m, slot(c), a], (y_dev, x_dev)[a])

    def z_send(m, c):
        for d in range(1, depth):
            z_copy(m, c, d).start()

    def xy_send(m, c):
        for d in range(1, depth):
            z_copy(m, c, d).wait_recv()
        for a in range(2):
            xy_copy(m, c, a).start()

    def f_send(m, c):
        for a in range(2):
            xy_copy(m, c, a).wait_recv()
            f_copy(m, c, a).start()

    def f_wait(m, c):
        for a in range(2):
            f_copy(m, c, a).wait_recv()

    def r1_copy(m, c, a):
        ref = part.at[m, c, (first_rows(across), last_rows(across))[a]]
        return send(ref, r1.at[m, c, a], r1s.at[m, c, a], r1r.at[m, c, a], (y_dev, x_dev)[a])

    def r2_copy(m, c, a):
        ref = part.at[m, c, bundle_rows((xn, yn)[a])]
        return send(ref, r2.at[m, c, a], r2s.at[m, c, a], r2r.at[m, c, a], (x_dev, y_dev)[a])

    def r3_copy(m, c, d):
        ref = zb.at[m, c, rows(peer(d) * tok_dev, tok_dev)]
        return send(ref, r3.at[m, c, d - 1], r3s.at[m, c, d - 1], r3r.at[m, c, d - 1], peer(d) * PLANE + yx)

    def relay_copy(m, c):
        return pltpu.make_async_remote_copy(
            src_ref=outb.at[m, c], dst_ref=cur.at[m, c], send_sem=cs.at[m, c], recv_sem=cr.at[m, c],
            device_id=(1 - seg, me), device_id_type=MESH,
        )

    f32 = jnp.float32

    def r2_send(m, c):
        for a in range(2):
            r1_copy(m, c, a).wait_recv()
            into = (first_rows(xn), last_rows(yn))[a]
            part[m, c, into] = (part[m, c, into].astype(f32) + r1[m, c, a].astype(f32)).astype(jnp.bfloat16)
            r2_copy(m, c, a).start()

    def r3_send(m, c):
        for a in range(2):
            r2_copy(m, c, a).wait_recv()
        total = part[m, c, bundle_rows(yx)].astype(f32) + r2[m, c, 0].astype(f32) + r2[m, c, 1].astype(f32)
        zb[m, c] = total.astype(jnp.bfloat16)
        for d in range(1, depth):
            r3_copy(m, c, d).start()

    def gather_sent(m, c):
        for d in range(1, depth):
            z_copy(m, c, d).wait_send()
        for a in range(2):
            xy_copy(m, c, a).wait_send()
            f_copy(m, c, a).wait_send()

    def finish(m, c):
        gather_sent(m, c)
        for a in range(2):
            r1_copy(m, c, a).wait_send()
            r2_copy(m, c, a).wait_send()
        for d in range(1, depth):
            r3_copy(m, c, d).wait_recv()
        inside = rows(z * tok_dev, tok_dev)
        total = part[m, c, own_rows].astype(f32) + r2[m, c, 0, inside].astype(f32) + r2[m, c, 1, inside].astype(f32)
        for d in range(1, depth):
            total = total + r3[m, c, d - 1].astype(f32)
        value = (cur[m, c].astype(f32) + total).astype(jnp.bfloat16)
        outb[m, c] = value
        out[m, :, pl.ds(pl.multiple_of(c * wide, LANES), wide)] = value

        @pl.when(seg == 0)
        def _():
            relay_copy(m, c).start()

    def weight_copy(which, c):
        src = (
            wg.at[rows(c * wide, wide)], wu.at[rows(c * wide, wide)],
            wd.at[:, pl.ds(pl.multiple_of(c * wide, LANES), wide)],
        )[which]
        return pltpu.make_async_copy(src, (wgv, wuv, wdv)[which].at[c], wsem.at[which, c])

    def up_chunk(m, c):
        f_wait(m, c)

        @pl.when(m == 0)
        def _():
            weight_copy(0, c).wait()
            weight_copy(1, c).wait()

        x = xg[m, c]
        gate = jnp.dot(x, wgv[c], preferred_element_type=f32)
        up = jnp.dot(x, wuv[c], preferred_element_type=f32)

        @pl.when(c == 0)
        def _():
            acc[0] = gate
            acc[1] = up

        @pl.when(c > 0)
        def _():
            acc[0] += gate
            acc[1] += up

    experts = groups

    def down_chunk(m, c):
        @pl.when(m == 0)
        def _():
            weight_copy(2, c).wait()

        lane = lax.broadcasted_iota(jnp.int32, (groups * tok_dev, LANES), 1)
        gate = jnp.sum(jnp.where(lane == m * experts + me, gb[...], 0.0), axis=1, keepdims=True)
        value = jnp.dot(hid[...], wdv[c], preferred_element_type=f32)
        part[m, c] = (value * gate).astype(jnp.bfloat16)
        for a in range(2):
            r1_copy(m, c, a).start()

    def take_in(m):
        @pl.when(seg == 0)
        def _():
            for c in range(chunks):
                cur[m, c] = tok[m, :, c * wide:(c + 1) * wide]

        @pl.when(seg > 0)
        def _():
            for c in range(chunks):
                relay_copy(m, c).wait_recv()

        square = jnp.zeros((tok_dev, 1), f32)
        for c in range(chunks):
            value = cur[m, c].astype(f32)
            square = square + jnp.sum(value * value, axis=1, keepdims=True)
        scale = lax.rsqrt(square / width + 1e-6)
        for c in range(chunks):
            value = cur[m, c].astype(f32) * scale * gain[:, c * wide:(c + 1) * wide]
            xg[m, c, own_rows] = value.astype(jnp.bfloat16)
            z_send(m, c)

    def hidden():
        gate = acc[0]
        hid[...] = (gate * jax.nn.sigmoid(gate) * acc[1]).astype(jnp.bfloat16)

    barrier = pltpu.get_barrier_semaphore()
    partners = [(seg, peer(d) * PLANE + yx) for d in range(1, depth)]
    partners += [(seg, x_dev), (seg, y_dev), (1 - seg, me)]
    for partner in partners:
        pl.semaphore_signal(barrier, inc=1, device_id=partner, device_id_type=MESH)
    for c in range(chunks):
        weight_copy(0, c).start()
        weight_copy(1, c).start()
    for c in range(chunks):
        weight_copy(2, c).start()

    row = lax.broadcasted_iota(jnp.int32, (LANES, tok_dev), 0)
    gates = jnp.zeros((LANES, tok_dev), f32)
    for m in range(micro):
        for k in range(ids.shape[1]):
            hit = row == ids[m, k:k + 1] + m * experts
            gates = gates + jnp.where(hit, gw[m, k:k + 1], 0.0)
    gb[own_rows] = gates.T
    pl.semaphore_wait(barrier, len(partners))

    take_in(0)
    z_send(0, None)

    def at(first, relayed):
        return first + (relayed - first) * seg

    n = chunks
    take_at = at(n - 2, n + 8)
    gates_at = n
    down_0 = n + 4
    down_1 = at(3 * n + 4, 2 * n + 14)
    fin_1 = at(3 * n + 12, 2 * n + 20)
    plan = (
        (r3_send, 0, n + 9), (r3_send, 1, at(3 * n + 9, 2 * n + 18)),
        (r2_send, 0, n + 6), (r2_send, 1, at(3 * n + 6, 2 * n + 16)),
        (xy_send, 0, 0), (xy_send, 1, at(n + 2, n + 10)),
        (f_send, 0, 2), (f_send, 1, at(n + 5, n + 12)),
        (finish, 0, n + 12), (finish, 1, fin_1),
        (up_chunk, 0, 4), (up_chunk, 1, at(2 * n + 4, n + 14)),
        (down_chunk, 0, down_0), (down_chunk, 1, down_1),
    )

    def step(s, carry):
        @pl.when(s == take_at)
        def _():
            take_in(1)

        @pl.when(s == gates_at)
        def _():
            xy_send(0, None)

        @pl.when(s == gates_at + 2)
        def _():
            f_send(0, None)

        @pl.when(s == down_0)
        def _():
            f_wait(0, None)
            hidden()

        @pl.when(s == down_1)
        def _():
            hidden()

        for action, m, first in plan:
            @pl.when((s >= first) & (s < first + chunks))
            def _(action=action, m=m, first=first):
                action(m, s - first)

        return carry

    lax.fori_loop(0, fin_1 + n, step, 0)

    def drain(i, carry):
        m = i // chunks
        c = i % chunks
        for d in range(1, depth):
            r3_copy(m, c, d).wait_send()

        @pl.when(seg == 0)
        def _():
            relay_copy(m, c).wait_send()

        return carry

    lax.fori_loop(0, micro * chunks, drain, 0)
    gather_sent(0, None)


def fused(tokens, expert_ids, gate_weights, norm_gain, w_gate, w_up, w_down):
    micro, tok_dev, width = tokens.shape
    ff = w_gate.shape[-1]
    groups = lax.axis_size("expert")
    segments = lax.axis_size("segment")
    depth = groups // PLANE
    rows = groups * tok_dev
    bundle = depth * tok_dev
    chunks = CHUNKS
    wide = width // chunks
    bf16 = jnp.bfloat16
    dma = pltpu.SemaphoreType.DMA
    vmem = pl.BlockSpec(memory_space=pltpu.VMEM)
    hbm = pl.BlockSpec(memory_space=pl.ANY)
    scratch = [
        pltpu.VMEM((micro, chunks, rows, wide), bf16),
        pltpu.VMEM((micro, chunks, tok_dev, wide), bf16),
        pltpu.VMEM((micro, chunks, tok_dev, wide), bf16),
        pltpu.VMEM((micro, chunks, rows, wide), bf16),
        pltpu.VMEM((micro, chunks, 2, bundle // 2, wide), bf16),
        pltpu.VMEM((micro, chunks, 2, bundle, wide), bf16),
        pltpu.VMEM((micro, chunks, depth - 1, tok_dev, wide), bf16),
        pltpu.VMEM((micro, chunks, bundle, wide), bf16),
        pltpu.VMEM((rows, LANES), jnp.float32),
        pltpu.VMEM((chunks, wide, ff), bf16),
        pltpu.VMEM((chunks, wide, ff), bf16),
        pltpu.VMEM((chunks, ff, wide), bf16),
        pltpu.VMEM((2, rows, ff), jnp.float32),
        pltpu.VMEM((rows, ff), bf16),
        dma((3, chunks)),
    ]
    for count, kinds in ((chunks + 1, (depth - 1, 2, 2)), (chunks, (2, 2, depth - 1))):
        for kind in kinds:
            scratch += [dma((micro, count, kind))] * 2
    scratch += [dma((micro, chunks))] * 2
    result = pl.pallas_call(
        functools.partial(relay_kernel, micro, segments, groups, tok_dev, width, ff, chunks),
        out_shape=jax.ShapeDtypeStruct((micro, tok_dev, width), bf16),
        in_specs=[vmem, vmem, vmem, vmem, hbm, hbm, hbm],
        out_specs=vmem,
        scratch_shapes=scratch,
        compiler_params=pltpu.CompilerParams(
            collective_id=0, has_side_effects=True, vmem_limit_bytes=VMEM_BYTES
        ),
        cost_estimate=pl.CostEstimate(
            flops=micro * 6 * rows * width * ff, bytes_accessed=3 * width * ff * 2, transcendentals=micro * rows * ff
        ),
    )(tokens, jnp.swapaxes(expert_ids[0], 1, 2), jnp.swapaxes(gate_weights[0], 1, 2), norm_gain, w_gate[0, 0], w_up[0, 0], w_down[0, 0])
    return result[None]


def fits(tokens, expert_ids, w_gate):
    micro, tok_dev, width = tokens.shape
    groups = lax.axis_size("expert")
    return (
        lax.axis_size("segment") == 2
        and w_gate.shape[1] == 1
        and groups % PLANE == 0
        and groups > PLANE
        and (groups // PLANE) % 2 == 0
        and tok_dev % 16 == 0
        and width % (CHUNKS * LANES) == 0
        and micro * groups <= LANES
        and vmem_need(micro, tok_dev, width, w_gate.shape[3], groups) < VMEM_BYTES * 4 // 5
    )


def from_behind(value, axis, steps):
    count = lax.axis_size(axis)
    initial, last = (max(0, -steps), min(count, count - steps))
    return lax.ppermute(value, axis, [(source, source + steps) for source in range(initial, last)])


def norm_rows(current, gain):
    values = current.astype(jnp.float32)
    scaled = values * lax.rsqrt(jnp.mean(values * values, axis=-1, keepdims=True) + 1e-06)
    return (scaled * gain).astype(jnp.bfloat16)


def slot_index(routes, capacity, experts):
    flat = routes.reshape(-1)
    onehot = (flat[:, None] == jnp.arange(experts, dtype=jnp.int32)[None, :]).astype(jnp.int32)
    ranks = jnp.sum(jnp.cumsum(onehot, axis=0) * onehot, axis=1) - 1
    return (flat * capacity + ranks).reshape(routes.shape)


def expert_rows(received, weights):
    gate_all, up_all, down_all = weights
    row_block = received[:, 0].reshape(-1, received.shape[-1])
    gate_part = jnp.dot(row_block, gate_all[0], preferred_element_type=jnp.float32)
    up_part = jnp.dot(row_block, up_all[0], preferred_element_type=jnp.float32)
    hidden = (jax.nn.silu(gate_part) * up_part).astype(jnp.bfloat16)
    result = jnp.dot(hidden, down_all[0], preferred_element_type=jnp.float32).astype(jnp.bfloat16)
    outputs = [result.reshape(received.shape[0], received.shape[2], received.shape[3])]
    return jnp.stack(outputs, axis=1)


def serve_rows(received, weights):
    return lax.all_to_all(
        expert_rows(received, weights), "expert", split_axis=0, concat_axis=0, tiled=True
    )


def pick_rows(gathered, all_routes, member, local, capacity, groups):
    tok_dev = all_routes.shape[0] // groups
    top = all_routes.shape[1]
    blocks = all_routes.reshape(groups, tok_dev * top)
    owners = member * local + jnp.arange(local, dtype=jnp.int32)
    counts = (blocks[:, :, None] == owners[None, None, :]).astype(jnp.int32)
    ranks = jnp.cumsum(counts, axis=1) * counts - 1
    hits = (ranks[..., None] == jnp.arange(capacity, dtype=jnp.int32)).astype(jnp.int32)
    selector = hits.reshape(groups, tok_dev, top, local, capacity).sum(axis=2).astype(jnp.bfloat16)
    features = gathered.reshape(groups, tok_dev, gathered.shape[-1])
    return jnp.einsum(
        "ntec,ntd->necd", selector, features, preferred_element_type=jnp.float32
    ).astype(jnp.bfloat16)


def shards(tokens, expert_ids, gate_weights, norm_gain, w_gate, w_up, w_down):
    if fits(tokens, expert_ids, w_gate):
        return fused(tokens, expert_ids, gate_weights, norm_gain, w_gate, w_up, w_down)
    micro = tokens.shape[0]
    tok_dev = tokens.shape[1]
    width = tokens.shape[2]
    top = expert_ids.shape[-1]
    groups = lax.axis_size("expert")
    segments = lax.axis_size("segment")
    local = w_gate.shape[1]
    experts = local * groups
    capacity = 2 * tok_dev * top // experts
    segment_no = lax.axis_index("segment")
    member = lax.axis_index("expert")
    gain = norm_gain[0]
    weights = (w_gate[0], w_up[0], w_down[0])
    incoming = jnp.zeros((tok_dev, width), jnp.bfloat16)
    results = jnp.zeros((micro, tok_dev, width), jnp.bfloat16)
    total_ticks = micro + segments - 1
    for tick_no in range(total_ticks):
        offset = tick_no - segment_no
        micro_no = jnp.clip(offset, 0, micro - 1)
        fresh = tokens[min(tick_no, micro - 1)]
        current = jnp.where(segment_no == 0, fresh, incoming)
        routes = lax.dynamic_index_in_dim(expert_ids[0], micro_no, 0, keepdims=False)
        weighting = lax.dynamic_index_in_dim(gate_weights[0], micro_no, 0, keepdims=False)
        normed = norm_rows(current, gain)
        places = slot_index(routes, capacity, experts)
        gathered, all_routes = (
            lax.all_gather(normed, "expert", axis=0, tiled=True),
            lax.all_gather(routes, "expert", axis=0, tiled=True),
        )
        returned = serve_rows(
            pick_rows(gathered, all_routes, member, local, capacity, groups), weights
        )
        flat_back = returned.reshape(-1, width)
        picked = jnp.take(flat_back, places.reshape(-1), axis=0).reshape(tok_dev, top, width)
        mixed = (
            current.astype(jnp.float32)
            + jnp.sum(weighting[:, :, None] * picked.astype(jnp.float32), axis=1)
        ).astype(jnp.bfloat16)
        valid = (offset >= 0) & (offset < micro)
        updated = lax.dynamic_update_index_in_dim(results, mixed, micro_no, 0)
        results = jnp.where(valid, updated, results)
        if tick_no < total_ticks - 1:
            incoming = from_behind(mixed, "segment", 1)
    return results[None]


def solution(mesh):
    in_specs = (
        P(None, "expert", None),
        P("segment", None, "expert", None),
        P("segment", None, "expert", None),
        P("segment", None),
        P("segment", "expert", None, None),
        P("segment", "expert", None, None),
        P("segment", "expert", None, None),
    )
    out_specs = P("segment", None, "expert", None)
    return jax.shard_map(shards, mesh=mesh, in_specs=in_specs, out_specs=out_specs, check_vma=False)
```

```python
import functools

import jax
import jax.numpy as jnp
from jax import lax
from jax.experimental import pallas as pl
from jax.experimental.pallas import tpu as pltpu
from jax.sharding import PartitionSpec as P

PLANE = 4
CHUNKS = 2
LANES = 128
VMEM_BYTES = 60 * 1024 * 1024
MESH = pl.DeviceIdType.MESH


def vmem_need(micro, tok_dev, width, ff, groups):
    rows = tok_dev * groups
    weights = 3 * width * ff * 2
    features = 2 * micro * rows * width * 2
    landing = micro * (rows // PLANE) * width * 2 * 4 + micro * tok_dev * width * 2 * 6
    hidden = rows * ff * (8 + 2) + rows * LANES * 4
    return weights + features + landing + hidden


def relay_kernel(
    micro, segments, groups, tok_dev, width, ff, chunks,
    tok, ids, gw, gain, wg, wu, wd, out,
    xg, cur, outb, part, r1, r2, r3, zb, gb, wgv, wuv, wdv, acc, hid,
    wsem, zs, zr, xs, xr, fs, fr, r1s, r1r, r2s, r2r, r3s, r3r, cs, cr,
):
    depth = groups // PLANE
    wide = width // chunks
    bundle = depth * tok_dev
    half = bundle // 2
    seg = lax.axis_index("segment")
    me = lax.axis_index("expert")
    yx = me % PLANE
    z = me // PLANE
    xn = yx + 1 - 2 * (yx % 2)
    yn = yx + 2 - 4 * (yx // 2)
    across = PLANE - 1 - yx
    x_dev = z * PLANE + xn
    y_dev = z * PLANE + yn

    def rows(start, size):
        return pl.ds(pl.multiple_of(start, 16), size)

    def peer(d):
        return (z + d) % depth

    own_rows = rows((yx * depth + z) * tok_dev, tok_dev)

    def bundle_rows(which):
        return rows(which * bundle, bundle)

    def first_rows(which):
        return rows(which * bundle, half)

    def last_rows(which):
        return rows(which * bundle + half, half)

    def send(src, dst, s, r, dev):
        return pltpu.make_async_remote_copy(
            src_ref=src, dst_ref=dst, send_sem=s, recv_sem=r, device_id=(seg, dev), device_id_type=MESH
        )

    def feature(m, c):
        return gb if c is None else xg.at[m, c]

    def slot(c):
        return chunks if c is None else c

    def z_copy(m, c, d):
        ref = feature(m, c).at[own_rows]
        return send(ref, ref, zs.at[m, slot(c), d - 1], zr.at[m, slot(c), d - 1], peer(d) * PLANE + yx)

    def xy_copy(m, c, a):
        ref = feature(m, c).at[bundle_rows(yx)]
        return send(ref, ref, xs.at[m, slot(c), a], xr.at[m, slot(c), a], (x_dev, y_dev)[a])

    def f_copy(m, c, a):
        ref = feature(m, c).at[(first_rows(xn), last_rows(yn))[a]]
        return send(ref, ref, fs.at[m, slot(c), a], fr.at[m, slot(c), a], (y_dev, x_dev)[a])

    def z_send(m, c):
        for d in range(1, depth):
            z_copy(m, c, d).start()

    def xy_send(m, c):
        for d in range(1, depth):
            z_copy(m, c, d).wait_recv()
        for a in range(2):
            xy_copy(m, c, a).start()

    def f_send(m, c):
        for a in range(2):
            xy_copy(m, c, a).wait_recv()
            f_copy(m, c, a).start()

    def f_wait(m, c):
        for a in range(2):
            f_copy(m, c, a).wait_recv()

    def r1_copy(m, c, a):
        ref = part.at[m, c, (first_rows(across), last_rows(across))[a]]
        return send(ref, r1.at[m, c, a], r1s.at[m, c, a], r1r.at[m, c, a], (y_dev, x_dev)[a])

    def r2_copy(m, c, a):
        ref = part.at[m, c, bundle_rows((xn, yn)[a])]
        return send(ref, r2.at[m, c, a], r2s.at[m, c, a], r2r.at[m, c, a], (x_dev, y_dev)[a])

    def r3_copy(m, c, d):
        ref = zb.at[m, c, rows(peer(d) * tok_dev, tok_dev)]
        return send(ref, r3.at[m, c, d - 1], r3s.at[m, c, d - 1], r3r.at[m, c, d - 1], peer(d) * PLANE + yx)

    def relay_copy(m, c):
        return pltpu.make_async_remote_copy(
            src_ref=outb.at[m, c], dst_ref=cur.at[m, c], send_sem=cs.at[m, c], recv_sem=cr.at[m, c],
            device_id=(1 - seg, me), device_id_type=MESH,
        )

    f32 = jnp.float32

    def r2_send(m, c):
        for a in range(2):
            r1_copy(m, c, a).wait_recv()
            into = (first_rows(xn), last_rows(yn))[a]
            part[m, c, into] = (part[m, c, into].astype(f32) + r1[m, c, a].astype(f32)).astype(jnp.bfloat16)
            r2_copy(m, c, a).start()

    def r3_send(m, c):
        for a in range(2):
            r2_copy(m, c, a).wait_recv()
        total = part[m, c, bundle_rows(yx)].astype(f32) + r2[m, c, 0].astype(f32) + r2[m, c, 1].astype(f32)
        zb[m, c] = total.astype(jnp.bfloat16)
        for d in range(1, depth):
            r3_copy(m, c, d).start()

    def gather_sent(m, c):
        for d in range(1, depth):
            z_copy(m, c, d).wait_send()
        for a in range(2):
            xy_copy(m, c, a).wait_send()
            f_copy(m, c, a).wait_send()

    def finish(m, c):
        gather_sent(m, c)
        for a in range(2):
            r1_copy(m, c, a).wait_send()
            r2_copy(m, c, a).wait_send()
        for d in range(1, depth):
            r3_copy(m, c, d).wait_recv()
        inside = rows(z * tok_dev, tok_dev)
        total = part[m, c, own_rows].astype(f32) + r2[m, c, 0, inside].astype(f32) + r2[m, c, 1, inside].astype(f32)
        for d in range(1, depth):
            total = total + r3[m, c, d - 1].astype(f32)
        value = (cur[m, c].astype(f32) + total).astype(jnp.bfloat16)
        outb[m, c] = value
        out[m, :, pl.ds(pl.multiple_of(c * wide, LANES), wide)] = value

        @pl.when(seg == 0)
        def _():
            relay_copy(m, c).start()

    def weight_copy(which, c):
        src = (
            wg.at[rows(c * wide, wide)], wu.at[rows(c * wide, wide)],
            wd.at[:, pl.ds(pl.multiple_of(c * wide, LANES), wide)],
        )[which]
        return pltpu.make_async_copy(src, (wgv, wuv, wdv)[which].at[c], wsem.at[which, c])

    def up_chunk(m, c):
        f_wait(m, c)

        @pl.when(m == 0)
        def _():
            weight_copy(0, c).wait()
            weight_copy(1, c).wait()

        x = xg[m, c]
        gate = jnp.dot(x, wgv[c], preferred_element_type=f32)
        up = jnp.dot(x, wuv[c], preferred_element_type=f32)

        @pl.when(c == 0)
        def _():
            acc[0] = gate
            acc[1] = up

        @pl.when(c > 0)
        def _():
            acc[0] += gate
            acc[1] += up

    experts = groups

    def down_chunk(m, c):
        @pl.when(m == 0)
        def _():
            weight_copy(2, c).wait()

        lane = lax.broadcasted_iota(jnp.int32, (groups * tok_dev, LANES), 1)
        gate = jnp.sum(jnp.where(lane == m * experts + me, gb[...], 0.0), axis=1, keepdims=True)
        value = jnp.dot(hid[...], wdv[c], preferred_element_type=f32)
        part[m, c] = (value * gate).astype(jnp.bfloat16)
        for a in range(2):
            r1_copy(m, c, a).start()

    def take_in(m):
        @pl.when(seg == 0)
        def _():
            for c in range(chunks):
                cur[m, c] = tok[m, :, c * wide:(c + 1) * wide]

        @pl.when(seg > 0)
        def _():
            for c in range(chunks):
                relay_copy(m, c).wait_recv()

        square = jnp.zeros((tok_dev, 1), f32)
        for c in range(chunks):
            value = cur[m, c].astype(f32)
            square = square + jnp.sum(value * value, axis=1, keepdims=True)
        scale = lax.rsqrt(square / width + 1e-6)
        for c in range(chunks):
            value = cur[m, c].astype(f32) * scale * gain[:, c * wide:(c + 1) * wide]
            xg[m, c, own_rows] = value.astype(jnp.bfloat16)
            z_send(m, c)

    def hidden():
        gate = acc[0]
        hid[...] = (gate * jax.nn.sigmoid(gate) * acc[1]).astype(jnp.bfloat16)

    barrier = pltpu.get_barrier_semaphore()
    partners = [(seg, peer(d) * PLANE + yx) for d in range(1, depth)]
    partners += [(seg, x_dev), (seg, y_dev), (1 - seg, me)]
    for partner in partners:
        pl.semaphore_signal(barrier, inc=1, device_id=partner, device_id_type=MESH)
    for c in range(chunks):
        weight_copy(0, c).start()
        weight_copy(1, c).start()
    for c in range(chunks):
        weight_copy(2, c).start()

    row = lax.broadcasted_iota(jnp.int32, (LANES, tok_dev), 0)
    gates = jnp.zeros((LANES, tok_dev), f32)
    for m in range(micro):
        for k in range(ids.shape[1]):
            hit = row == ids[m, k:k + 1] + m * experts
            gates = gates + jnp.where(hit, gw[m, k:k + 1], 0.0)
    gb[own_rows] = gates.T
    pl.semaphore_wait(barrier, len(partners))

    take_in(0)
    z_send(0, None)

    def at(first, relayed):
        return first + (relayed - first) * seg

    n = chunks
    take_at = at(n - 1, n + 8)
    gates_at = n
    down_0 = n + 4
    down_1 = at(3 * n + 4, 2 * n + 14)
    fin_1 = at(3 * n + 10, 2 * n + 20)
    plan = (
        (r3_send, 0, n + 8), (r3_send, 1, at(3 * n + 8, 2 * n + 18)),
        (r2_send, 0, n + 6), (r2_send, 1, at(3 * n + 6, 2 * n + 16)),
        (xy_send, 0, 0), (xy_send, 1, at(n + 2, n + 10)),
        (f_send, 0, 2), (f_send, 1, at(n + 5, n + 12)),
        (finish, 0, n + 10), (finish, 1, fin_1),
        (up_chunk, 0, 4), (up_chunk, 1, at(2 * n + 4, n + 14)),
        (down_chunk, 0, down_0), (down_chunk, 1, down_1),
    )

    def step(s, carry):
        @pl.when(s == take_at)
        def _():
            take_in(1)

        @pl.when(s == gates_at)
        def _():
            xy_send(0, None)

        @pl.when(s == gates_at + 2)
        def _():
            f_send(0, None)

        @pl.when(s == down_0)
        def _():
            f_wait(0, None)
            hidden()

        @pl.when(s == down_1)
        def _():
            hidden()

        for action, m, first in plan:
            @pl.when((s >= first) & (s < first + chunks))
            def _(action=action, m=m, first=first):
                action(m, s - first)

        return carry

    lax.fori_loop(0, fin_1 + n, step, 0)

    def drain(i, carry):
        m = i // chunks
        c = i % chunks
        for d in range(1, depth):
            r3_copy(m, c, d).wait_send()

        @pl.when(seg == 0)
        def _():
            relay_copy(m, c).wait_send()

        return carry

    lax.fori_loop(0, micro * chunks, drain, 0)
    gather_sent(0, None)


def fused(tokens, expert_ids, gate_weights, norm_gain, w_gate, w_up, w_down):
    micro, tok_dev, width = tokens.shape
    ff = w_gate.shape[-1]
    groups = lax.axis_size("expert")
    segments = lax.axis_size("segment")
    depth = groups // PLANE
    rows = groups * tok_dev
    bundle = depth * tok_dev
    chunks = CHUNKS
    wide = width // chunks
    bf16 = jnp.bfloat16
    dma = pltpu.SemaphoreType.DMA
    vmem = pl.BlockSpec(memory_space=pltpu.VMEM)
    hbm = pl.BlockSpec(memory_space=pl.ANY)
    scratch = [
        pltpu.VMEM((micro, chunks, rows, wide), bf16),
        pltpu.VMEM((micro, chunks, tok_dev, wide), bf16),
        pltpu.VMEM((micro, chunks, tok_dev, wide), bf16),
        pltpu.VMEM((micro, chunks, rows, wide), bf16),
        pltpu.VMEM((micro, chunks, 2, bundle // 2, wide), bf16),
        pltpu.VMEM((micro, chunks, 2, bundle, wide), bf16),
        pltpu.VMEM((micro, chunks, depth - 1, tok_dev, wide), bf16),
        pltpu.VMEM((micro, chunks, bundle, wide), bf16),
        pltpu.VMEM((rows, LANES), jnp.float32),
        pltpu.VMEM((chunks, wide, ff), bf16),
        pltpu.VMEM((chunks, wide, ff), bf16),
        pltpu.VMEM((chunks, ff, wide), bf16),
        pltpu.VMEM((2, rows, ff), jnp.float32),
        pltpu.VMEM((rows, ff), bf16),
        dma((3, chunks)),
    ]
    for count, kinds in ((chunks + 1, (depth - 1, 2, 2)), (chunks, (2, 2, depth - 1))):
        for kind in kinds:
            scratch += [dma((micro, count, kind))] * 2
    scratch += [dma((micro, chunks))] * 2
    result = pl.pallas_call(
        functools.partial(relay_kernel, micro, segments, groups, tok_dev, width, ff, chunks),
        out_shape=jax.ShapeDtypeStruct((micro, tok_dev, width), bf16),
        in_specs=[vmem, vmem, vmem, vmem, hbm, hbm, hbm],
        out_specs=vmem,
        scratch_shapes=scratch,
        compiler_params=pltpu.CompilerParams(
            collective_id=0, has_side_effects=True, vmem_limit_bytes=VMEM_BYTES
        ),
        cost_estimate=pl.CostEstimate(
            flops=micro * 6 * rows * width * ff, bytes_accessed=3 * width * ff * 2, transcendentals=micro * rows * ff
        ),
    )(tokens, jnp.swapaxes(expert_ids[0], 1, 2), jnp.swapaxes(gate_weights[0], 1, 2), norm_gain, w_gate[0, 0], w_up[0, 0], w_down[0, 0])
    return result[None]


def fits(tokens, expert_ids, w_gate):
    micro, tok_dev, width = tokens.shape
    groups = lax.axis_size("expert")
    return (
        lax.axis_size("segment") == 2
        and w_gate.shape[1] == 1
        and groups % PLANE == 0
        and groups > PLANE
        and (groups // PLANE) % 2 == 0
        and tok_dev % 16 == 0
        and width % (CHUNKS * LANES) == 0
        and micro * groups <= LANES
        and vmem_need(micro, tok_dev, width, w_gate.shape[3], groups) < VMEM_BYTES * 4 // 5
    )


def from_behind(value, axis, steps):
    count = lax.axis_size(axis)
    initial, last = (max(0, -steps), min(count, count - steps))
    return lax.ppermute(value, axis, [(source, source + steps) for source in range(initial, last)])


def norm_rows(current, gain):
    values = current.astype(jnp.float32)
    scaled = values * lax.rsqrt(jnp.mean(values * values, axis=-1, keepdims=True) + 1e-06)
    return (scaled * gain).astype(jnp.bfloat16)


def slot_index(routes, capacity, experts):
    flat = routes.reshape(-1)
    onehot = (flat[:, None] == jnp.arange(experts, dtype=jnp.int32)[None, :]).astype(jnp.int32)
    ranks = jnp.sum(jnp.cumsum(onehot, axis=0) * onehot, axis=1) - 1
    return (flat * capacity + ranks).reshape(routes.shape)


def expert_rows(received, weights):
    gate_all, up_all, down_all = weights
    row_block = received[:, 0].reshape(-1, received.shape[-1])
    gate_part = jnp.dot(row_block, gate_all[0], preferred_element_type=jnp.float32)
    up_part = jnp.dot(row_block, up_all[0], preferred_element_type=jnp.float32)
    hidden = (jax.nn.silu(gate_part) * up_part).astype(jnp.bfloat16)
    result = jnp.dot(hidden, down_all[0], preferred_element_type=jnp.float32).astype(jnp.bfloat16)
    outputs = [result.reshape(received.shape[0], received.shape[2], received.shape[3])]
    return jnp.stack(outputs, axis=1)


def serve_rows(received, weights):
    return lax.all_to_all(
        expert_rows(received, weights), "expert", split_axis=0, concat_axis=0, tiled=True
    )


def pick_rows(gathered, all_routes, member, local, capacity, groups):
    tok_dev = all_routes.shape[0] // groups
    top = all_routes.shape[1]
    blocks = all_routes.reshape(groups, tok_dev * top)
    owners = member * local + jnp.arange(local, dtype=jnp.int32)
    counts = (blocks[:, :, None] == owners[None, None, :]).astype(jnp.int32)
    ranks = jnp.cumsum(counts, axis=1) * counts - 1
    hits = (ranks[..., None] == jnp.arange(capacity, dtype=jnp.int32)).astype(jnp.int32)
    selector = hits.reshape(groups, tok_dev, top, local, capacity).sum(axis=2).astype(jnp.bfloat16)
    features = gathered.reshape(groups, tok_dev, gathered.shape[-1])
    return jnp.einsum(
        "ntec,ntd->necd", selector, features, preferred_element_type=jnp.float32
    ).astype(jnp.bfloat16)


def shards(tokens, expert_ids, gate_weights, norm_gain, w_gate, w_up, w_down):
    if fits(tokens, expert_ids, w_gate):
        return fused(tokens, expert_ids, gate_weights, norm_gain, w_gate, w_up, w_down)
    micro = tokens.shape[0]
    tok_dev = tokens.shape[1]
    width = tokens.shape[2]
    top = expert_ids.shape[-1]
    groups = lax.axis_size("expert")
    segments = lax.axis_size("segment")
    local = w_gate.shape[1]
    experts = local * groups
    capacity = 2 * tok_dev * top // experts
    segment_no = lax.axis_index("segment")
    member = lax.axis_index("expert")
    gain = norm_gain[0]
    weights = (w_gate[0], w_up[0], w_down[0])
    incoming = jnp.zeros((tok_dev, width), jnp.bfloat16)
    results = jnp.zeros((micro, tok_dev, width), jnp.bfloat16)
    total_ticks = micro + segments - 1
    for tick_no in range(total_ticks):
        offset = tick_no - segment_no
        micro_no = jnp.clip(offset, 0, micro - 1)
        fresh = tokens[min(tick_no, micro - 1)]
        current = jnp.where(segment_no == 0, fresh, incoming)
        routes = lax.dynamic_index_in_dim(expert_ids[0], micro_no, 0, keepdims=False)
        weighting = lax.dynamic_index_in_dim(gate_weights[0], micro_no, 0, keepdims=False)
        normed = norm_rows(current, gain)
        places = slot_index(routes, capacity, experts)
        gathered, all_routes = (
            lax.all_gather(normed, "expert", axis=0, tiled=True),
            lax.all_gather(routes, "expert", axis=0, tiled=True),
        )
        returned = serve_rows(
            pick_rows(gathered, all_routes, member, local, capacity, groups), weights
        )
        flat_back = returned.reshape(-1, width)
        picked = jnp.take(flat_back, places.reshape(-1), axis=0).reshape(tok_dev, top, width)
        mixed = (
            current.astype(jnp.float32)
            + jnp.sum(weighting[:, :, None] * picked.astype(jnp.float32), axis=1)
        ).astype(jnp.bfloat16)
        valid = (offset >= 0) & (offset < micro)
        updated = lax.dynamic_update_index_in_dim(results, mixed, micro_no, 0)
        results = jnp.where(valid, updated, results)
        if tick_no < total_ticks - 1:
            incoming = from_behind(mixed, "segment", 1)
    return results[None]


def solution(mesh):
    in_specs = (
        P(None, "expert", None),
        P("segment", None, "expert", None),
        P("segment", None, "expert", None),
        P("segment", None),
        P("segment", "expert", None, None),
        P("segment", "expert", None, None),
        P("segment", "expert", None, None),
    )
    out_specs = P("segment", None, "expert", None)
    return jax.shard_map(shards, mesh=mesh, in_specs=in_specs, out_specs=out_specs, check_vma=False)
```

```python
import functools

import jax
import jax.numpy as jnp
from jax import lax
from jax.experimental import pallas as pl
from jax.experimental.pallas import tpu as pltpu
from jax.sharding import PartitionSpec as P

PLANE = 4
CHUNKS = 4
LANES = 128
VMEM_BYTES = 60 * 1024 * 1024
MESH = pl.DeviceIdType.MESH


def vmem_need(micro, tok_dev, width, ff, groups):
    rows = tok_dev * groups
    weights = 3 * width * ff * 2
    features = 2 * micro * rows * width * 2
    landing = micro * (rows // PLANE) * width * 2 * 4 + micro * tok_dev * width * 2 * 6
    hidden = rows * ff * (8 + 2) + rows * LANES * 4
    return weights + features + landing + hidden


def relay_kernel(
    micro, segments, groups, tok_dev, width, ff, chunks,
    tok, ids, gw, gain, wg, wu, wd, out,
    xg, cur, outb, part, r1, r2, r3, zb, gb, wgv, wuv, wdv, acc, hid,
    wsem, zs, zr, xs, xr, fs, fr, r1s, r1r, r2s, r2r, r3s, r3r, cs, cr,
):
    depth = groups // PLANE
    wide = width // chunks
    bundle = depth * tok_dev
    half = bundle // 2
    seg = lax.axis_index("segment")
    me = lax.axis_index("expert")
    yx = me % PLANE
    z = me // PLANE
    xn = yx + 1 - 2 * (yx % 2)
    yn = yx + 2 - 4 * (yx // 2)
    across = PLANE - 1 - yx
    x_dev = z * PLANE + xn
    y_dev = z * PLANE + yn

    def rows(start, size):
        return pl.ds(pl.multiple_of(start, 16), size)

    def peer(d):
        return (z + d) % depth

    own_rows = rows((yx * depth + z) * tok_dev, tok_dev)

    def bundle_rows(which):
        return rows(which * bundle, bundle)

    def first_rows(which):
        return rows(which * bundle, half)

    def last_rows(which):
        return rows(which * bundle + half, half)

    def send(src, dst, s, r, dev):
        return pltpu.make_async_remote_copy(
            src_ref=src, dst_ref=dst, send_sem=s, recv_sem=r, device_id=(seg, dev), device_id_type=MESH
        )

    def feature(m, c):
        return gb if c is None else xg.at[m, c]

    def slot(c):
        return chunks if c is None else c

    def z_copy(m, c, d):
        ref = feature(m, c).at[own_rows]
        return send(ref, ref, zs.at[m, slot(c), d - 1], zr.at[m, slot(c), d - 1], peer(d) * PLANE + yx)

    def xy_copy(m, c, a):
        ref = feature(m, c).at[bundle_rows(yx)]
        return send(ref, ref, xs.at[m, slot(c), a], xr.at[m, slot(c), a], (x_dev, y_dev)[a])

    def f_copy(m, c, a):
        ref = feature(m, c).at[(first_rows(xn), last_rows(yn))[a]]
        return send(ref, ref, fs.at[m, slot(c), a], fr.at[m, slot(c), a], (y_dev, x_dev)[a])

    def z_send(m, c):
        for d in range(1, depth):
            z_copy(m, c, d).start()

    def xy_send(m, c):
        for d in range(1, depth):
            z_copy(m, c, d).wait_recv()
        for a in range(2):
            xy_copy(m, c, a).start()

    def f_send(m, c):
        for a in range(2):
            xy_copy(m, c, a).wait_recv()
            f_copy(m, c, a).start()

    def f_wait(m, c):
        for a in range(2):
            f_copy(m, c, a).wait_recv()

    def r1_copy(m, c, a):
        ref = part.at[m, c, (first_rows(across), last_rows(across))[a]]
        return send(ref, r1.at[m, c, a], r1s.at[m, c, a], r1r.at[m, c, a], (y_dev, x_dev)[a])

    def r2_copy(m, c, a):
        ref = part.at[m, c, bundle_rows((xn, yn)[a])]
        return send(ref, r2.at[m, c, a], r2s.at[m, c, a], r2r.at[m, c, a], (x_dev, y_dev)[a])

    def r3_copy(m, c, d):
        ref = zb.at[m, c, rows(peer(d) * tok_dev, tok_dev)]
        return send(ref, r3.at[m, c, d - 1], r3s.at[m, c, d - 1], r3r.at[m, c, d - 1], peer(d) * PLANE + yx)

    def relay_copy(m, c):
        return pltpu.make_async_remote_copy(
            src_ref=outb.at[m, c], dst_ref=cur.at[m, c], send_sem=cs.at[m, c], recv_sem=cr.at[m, c],
            device_id=(1 - seg, me), device_id_type=MESH,
        )

    f32 = jnp.float32

    def r2_send(m, c):
        for a in range(2):
            r1_copy(m, c, a).wait_recv()
            into = (first_rows(xn), last_rows(yn))[a]
            part[m, c, into] = (part[m, c, into].astype(f32) + r1[m, c, a].astype(f32)).astype(jnp.bfloat16)
            r2_copy(m, c, a).start()

    def r3_send(m, c):
        for a in range(2):
            r2_copy(m, c, a).wait_recv()
        total = part[m, c, bundle_rows(yx)].astype(f32) + r2[m, c, 0].astype(f32) + r2[m, c, 1].astype(f32)
        zb[m, c] = total.astype(jnp.bfloat16)
        for d in range(1, depth):
            r3_copy(m, c, d).start()

    def gather_sent(m, c):
        for d in range(1, depth):
            z_copy(m, c, d).wait_send()
        for a in range(2):
            xy_copy(m, c, a).wait_send()
            f_copy(m, c, a).wait_send()

    def finish(m, c):
        gather_sent(m, c)
        for a in range(2):
            r1_copy(m, c, a).wait_send()
            r2_copy(m, c, a).wait_send()
        for d in range(1, depth):
            r3_copy(m, c, d).wait_recv()
        inside = rows(z * tok_dev, tok_dev)
        total = part[m, c, own_rows].astype(f32) + r2[m, c, 0, inside].astype(f32) + r2[m, c, 1, inside].astype(f32)
        for d in range(1, depth):
            total = total + r3[m, c, d - 1].astype(f32)
        value = (cur[m, c].astype(f32) + total).astype(jnp.bfloat16)
        outb[m, c] = value
        out[m, :, pl.ds(pl.multiple_of(c * wide, LANES), wide)] = value

        @pl.when(seg == 0)
        def _():
            relay_copy(m, c).start()

    def weight_copy(which, c):
        src = (
            wg.at[rows(c * wide, wide)], wu.at[rows(c * wide, wide)],
            wd.at[:, pl.ds(pl.multiple_of(c * wide, LANES), wide)],
        )[which]
        return pltpu.make_async_copy(src, (wgv, wuv, wdv)[which].at[c], wsem.at[which, c])

    def up_chunk(m, c):
        f_wait(m, c)

        @pl.when(m == 0)
        def _():
            weight_copy(0, c).wait()
            weight_copy(1, c).wait()

        x = xg[m, c]
        gate = jnp.dot(x, wgv[c], preferred_element_type=f32)
        up = jnp.dot(x, wuv[c], preferred_element_type=f32)

        @pl.when(c == 0)
        def _():
            acc[0] = gate
            acc[1] = up

        @pl.when(c > 0)
        def _():
            acc[0] += gate
            acc[1] += up

    experts = groups

    def down_chunk(m, c):
        @pl.when(m == 0)
        def _():
            weight_copy(2, c).wait()

        lane = lax.broadcasted_iota(jnp.int32, (groups * tok_dev, LANES), 1)
        gate = jnp.sum(jnp.where(lane == m * experts + me, gb[...], 0.0), axis=1, keepdims=True)
        value = jnp.dot(hid[...], wdv[c], preferred_element_type=f32)
        part[m, c] = (value * gate).astype(jnp.bfloat16)
        for a in range(2):
            r1_copy(m, c, a).start()

    def take_in(m):
        @pl.when(seg == 0)
        def _():
            for c in range(chunks):
                cur[m, c] = tok[m, :, c * wide:(c + 1) * wide]

        @pl.when(seg > 0)
        def _():
            for c in range(chunks):
                relay_copy(m, c).wait_recv()

        square = jnp.zeros((tok_dev, 1), f32)
        for c in range(chunks):
            value = cur[m, c].astype(f32)
            square = square + jnp.sum(value * value, axis=1, keepdims=True)
        scale = lax.rsqrt(square / width + 1e-6)
        for c in range(chunks):
            value = cur[m, c].astype(f32) * scale * gain[:, c * wide:(c + 1) * wide]
            xg[m, c, own_rows] = value.astype(jnp.bfloat16)
            z_send(m, c)

    def hidden():
        gate = acc[0]
        hid[...] = (gate * jax.nn.sigmoid(gate) * acc[1]).astype(jnp.bfloat16)

    barrier = pltpu.get_barrier_semaphore()
    partners = [(seg, peer(d) * PLANE + yx) for d in range(1, depth)]
    partners += [(seg, x_dev), (seg, y_dev), (1 - seg, me)]
    for partner in partners:
        pl.semaphore_signal(barrier, inc=1, device_id=partner, device_id_type=MESH)
    for c in range(chunks):
        weight_copy(0, c).start()
        weight_copy(1, c).start()
    for c in range(chunks):
        weight_copy(2, c).start()

    row = lax.broadcasted_iota(jnp.int32, (LANES, tok_dev), 0)
    gates = jnp.zeros((LANES, tok_dev), f32)
    for m in range(micro):
        for k in range(ids.shape[1]):
            hit = row == ids[m, k:k + 1] + m * experts
            gates = gates + jnp.where(hit, gw[m, k:k + 1], 0.0)
    gb[own_rows] = gates.T
    pl.semaphore_wait(barrier, len(partners))

    take_in(0)
    z_send(0, None)

    def at(first, relayed):
        return first + (relayed - first) * seg

    n = chunks
    take_at = at(n - 2, n + 8)
    gates_at = n
    down_0 = n + 4
    down_1 = at(3 * n + 4, 2 * n + 14)
    fin_1 = at(3 * n + 10, 2 * n + 20)
    plan = (
        (r3_send, 0, n + 8), (r3_send, 1, at(3 * n + 8, 2 * n + 18)),
        (r2_send, 0, n + 6), (r2_send, 1, at(3 * n + 6, 2 * n + 16)),
        (xy_send, 0, 0), (xy_send, 1, at(n + 2, n + 10)),
        (f_send, 0, 2), (f_send, 1, at(n + 5, n + 12)),
        (finish, 0, n + 10), (finish, 1, fin_1),
        (up_chunk, 0, 4), (up_chunk, 1, at(2 * n + 4, n + 14)),
        (down_chunk, 0, down_0), (down_chunk, 1, down_1),
    )

    def step(s, carry):
        @pl.when(s == take_at)
        def _():
            take_in(1)

        @pl.when(s == gates_at)
        def _():
            xy_send(0, None)

        @pl.when(s == gates_at + 2)
        def _():
            f_send(0, None)

        @pl.when(s == down_0)
        def _():
            f_wait(0, None)
            hidden()

        @pl.when(s == down_1)
        def _():
            hidden()

        for action, m, first in plan:
            @pl.when((s >= first) & (s < first + chunks))
            def _(action=action, m=m, first=first):
                action(m, s - first)

        return carry

    lax.fori_loop(0, fin_1 + n, step, 0)

    def drain(i, carry):
        m = i // chunks
        c = i % chunks
        for d in range(1, depth):
            r3_copy(m, c, d).wait_send()

        @pl.when(seg == 0)
        def _():
            relay_copy(m, c).wait_send()

        return carry

    lax.fori_loop(0, micro * chunks, drain, 0)
    gather_sent(0, None)


def fused(tokens, expert_ids, gate_weights, norm_gain, w_gate, w_up, w_down):
    micro, tok_dev, width = tokens.shape
    ff = w_gate.shape[-1]
    groups = lax.axis_size("expert")
    segments = lax.axis_size("segment")
    depth = groups // PLANE
    rows = groups * tok_dev
    bundle = depth * tok_dev
    chunks = CHUNKS
    wide = width // chunks
    bf16 = jnp.bfloat16
    dma = pltpu.SemaphoreType.DMA
    vmem = pl.BlockSpec(memory_space=pltpu.VMEM)
    hbm = pl.BlockSpec(memory_space=pl.ANY)
    scratch = [
        pltpu.VMEM((micro, chunks, rows, wide), bf16),
        pltpu.VMEM((micro, chunks, tok_dev, wide), bf16),
        pltpu.VMEM((micro, chunks, tok_dev, wide), bf16),
        pltpu.VMEM((micro, chunks, rows, wide), bf16),
        pltpu.VMEM((micro, chunks, 2, bundle // 2, wide), bf16),
        pltpu.VMEM((micro, chunks, 2, bundle, wide), bf16),
        pltpu.VMEM((micro, chunks, depth - 1, tok_dev, wide), bf16),
        pltpu.VMEM((micro, chunks, bundle, wide), bf16),
        pltpu.VMEM((rows, LANES), jnp.float32),
        pltpu.VMEM((chunks, wide, ff), bf16),
        pltpu.VMEM((chunks, wide, ff), bf16),
        pltpu.VMEM((chunks, ff, wide), bf16),
        pltpu.VMEM((2, rows, ff), jnp.float32),
        pltpu.VMEM((rows, ff), bf16),
        dma((3, chunks)),
    ]
    for count, kinds in ((chunks + 1, (depth - 1, 2, 2)), (chunks, (2, 2, depth - 1))):
        for kind in kinds:
            scratch += [dma((micro, count, kind))] * 2
    scratch += [dma((micro, chunks))] * 2
    result = pl.pallas_call(
        functools.partial(relay_kernel, micro, segments, groups, tok_dev, width, ff, chunks),
        out_shape=jax.ShapeDtypeStruct((micro, tok_dev, width), bf16),
        in_specs=[vmem, vmem, vmem, vmem, hbm, hbm, hbm],
        out_specs=vmem,
        scratch_shapes=scratch,
        compiler_params=pltpu.CompilerParams(
            collective_id=0, has_side_effects=True, vmem_limit_bytes=VMEM_BYTES
        ),
        cost_estimate=pl.CostEstimate(
            flops=micro * 6 * rows * width * ff, bytes_accessed=3 * width * ff * 2, transcendentals=micro * rows * ff
        ),
    )(tokens, jnp.swapaxes(expert_ids[0], 1, 2), jnp.swapaxes(gate_weights[0], 1, 2), norm_gain, w_gate[0, 0], w_up[0, 0], w_down[0, 0])
    return result[None]


def fits(tokens, expert_ids, w_gate):
    micro, tok_dev, width = tokens.shape
    groups = lax.axis_size("expert")
    return (
        lax.axis_size("segment") == 2
        and w_gate.shape[1] == 1
        and groups % PLANE == 0
        and groups > PLANE
        and (groups // PLANE) % 2 == 0
        and tok_dev % 16 == 0
        and width % (CHUNKS * LANES) == 0
        and micro * groups <= LANES
        and vmem_need(micro, tok_dev, width, w_gate.shape[3], groups) < VMEM_BYTES * 4 // 5
    )


def from_behind(value, axis, steps):
    count = lax.axis_size(axis)
    initial, last = (max(0, -steps), min(count, count - steps))
    return lax.ppermute(value, axis, [(source, source + steps) for source in range(initial, last)])


def norm_rows(current, gain):
    values = current.astype(jnp.float32)
    scaled = values * lax.rsqrt(jnp.mean(values * values, axis=-1, keepdims=True) + 1e-06)
    return (scaled * gain).astype(jnp.bfloat16)


def slot_index(routes, capacity, experts):
    flat = routes.reshape(-1)
    onehot = (flat[:, None] == jnp.arange(experts, dtype=jnp.int32)[None, :]).astype(jnp.int32)
    ranks = jnp.sum(jnp.cumsum(onehot, axis=0) * onehot, axis=1) - 1
    return (flat * capacity + ranks).reshape(routes.shape)


def expert_rows(received, weights):
    gate_all, up_all, down_all = weights
    row_block = received[:, 0].reshape(-1, received.shape[-1])
    gate_part = jnp.dot(row_block, gate_all[0], preferred_element_type=jnp.float32)
    up_part = jnp.dot(row_block, up_all[0], preferred_element_type=jnp.float32)
    hidden = (jax.nn.silu(gate_part) * up_part).astype(jnp.bfloat16)
    result = jnp.dot(hidden, down_all[0], preferred_element_type=jnp.float32).astype(jnp.bfloat16)
    outputs = [result.reshape(received.shape[0], received.shape[2], received.shape[3])]
    return jnp.stack(outputs, axis=1)


def serve_rows(received, weights):
    return lax.all_to_all(
        expert_rows(received, weights), "expert", split_axis=0, concat_axis=0, tiled=True
    )


def pick_rows(gathered, all_routes, member, local, capacity, groups):
    tok_dev = all_routes.shape[0] // groups
    top = all_routes.shape[1]
    blocks = all_routes.reshape(groups, tok_dev * top)
    owners = member * local + jnp.arange(local, dtype=jnp.int32)
    counts = (blocks[:, :, None] == owners[None, None, :]).astype(jnp.int32)
    ranks = jnp.cumsum(counts, axis=1) * counts - 1
    hits = (ranks[..., None] == jnp.arange(capacity, dtype=jnp.int32)).astype(jnp.int32)
    selector = hits.reshape(groups, tok_dev, top, local, capacity).sum(axis=2).astype(jnp.bfloat16)
    features = gathered.reshape(groups, tok_dev, gathered.shape[-1])
    return jnp.einsum(
        "ntec,ntd->necd", selector, features, preferred_element_type=jnp.float32
    ).astype(jnp.bfloat16)


def shards(tokens, expert_ids, gate_weights, norm_gain, w_gate, w_up, w_down):
    if fits(tokens, expert_ids, w_gate):
        return fused(tokens, expert_ids, gate_weights, norm_gain, w_gate, w_up, w_down)
    micro = tokens.shape[0]
    tok_dev = tokens.shape[1]
    width = tokens.shape[2]
    top = expert_ids.shape[-1]
    groups = lax.axis_size("expert")
    segments = lax.axis_size("segment")
    local = w_gate.shape[1]
    experts = local * groups
    capacity = 2 * tok_dev * top // experts
    segment_no = lax.axis_index("segment")
    member = lax.axis_index("expert")
    gain = norm_gain[0]
    weights = (w_gate[0], w_up[0], w_down[0])
    incoming = jnp.zeros((tok_dev, width), jnp.bfloat16)
    results = jnp.zeros((micro, tok_dev, width), jnp.bfloat16)
    total_ticks = micro + segments - 1
    for tick_no in range(total_ticks):
        offset = tick_no - segment_no
        micro_no = jnp.clip(offset, 0, micro - 1)
        fresh = tokens[min(tick_no, micro - 1)]
        current = jnp.where(segment_no == 0, fresh, incoming)
        routes = lax.dynamic_index_in_dim(expert_ids[0], micro_no, 0, keepdims=False)
        weighting = lax.dynamic_index_in_dim(gate_weights[0], micro_no, 0, keepdims=False)
        normed = norm_rows(current, gain)
        places = slot_index(routes, capacity, experts)
        gathered, all_routes = (
            lax.all_gather(normed, "expert", axis=0, tiled=True),
            lax.all_gather(routes, "expert", axis=0, tiled=True),
        )
        returned = serve_rows(
            pick_rows(gathered, all_routes, member, local, capacity, groups), weights
        )
        flat_back = returned.reshape(-1, width)
        picked = jnp.take(flat_back, places.reshape(-1), axis=0).reshape(tok_dev, top, width)
        mixed = (
            current.astype(jnp.float32)
            + jnp.sum(weighting[:, :, None] * picked.astype(jnp.float32), axis=1)
        ).astype(jnp.bfloat16)
        valid = (offset >= 0) & (offset < micro)
        updated = lax.dynamic_update_index_in_dim(results, mixed, micro_no, 0)
        results = jnp.where(valid, updated, results)
        if tick_no < total_ticks - 1:
            incoming = from_behind(mixed, "segment", 1)
    return results[None]


def solution(mesh):
    in_specs = (
        P(None, "expert", None),
        P("segment", None, "expert", None),
        P("segment", None, "expert", None),
        P("segment", None),
        P("segment", "expert", None, None),
        P("segment", "expert", None, None),
        P("segment", "expert", None, None),
    )
    out_specs = P("segment", None, "expert", None)
    return jax.shard_map(shards, mesh=mesh, in_specs=in_specs, out_specs=out_specs, check_vma=False)
```
